512 devices in a mesh: subj: 16 (over y_lo, x), depth: 32 (over y_hi, z, core).
Axes of the slice: x: 4, y: 8 (y_hi: 2, y_lo: 4; y = y_hi * 4 + y_lo), z: 8, core: 2. Of those that a mesh axis runs over, the one named last changes fastest.
Arguments:
- images: float32 [16, 160, 128, 128], P('subj', 'depth'), may hold values from -6 to 6
- velocity: float32 [3, 16, 160, 128, 128], P(None, 'subj', 'depth'), may hold values from -3 to 3
- ref_index: int32 [4], replicated, may hold values from 0 to 15
- ref_weights: int32 [16, 4], P('subj'), may hold values from 0 to 16
Outputs:
- velocity_out: float32 [3, 16, 160, 128, 128], P(None, 'subj', 'depth')
The draws below stay inside these ranges and needn't reach their ends.
Inputs may be any that keep to these rules, and one draw needn't show every extreme that they name: `ref_index`: subject indices of the references; they may repeat. `ref_weights`: numerators over 16.
All inputs are finite; a program needn't handle non-finite values.
Results may differ from the reference program's by a relative error of at most 0.0003.
Values sent between devices are 32-bit elements; how exact they have to be, the bound alone decides.
A program may use at most 64 MiB of HBM per device.

```python
import math
import jax
import jax.numpy as jnp
from jax import lax

X = 128
Y = 128
NREF = 4
WIN = 9
RG = 3
WDEN = 16
SUBJECTS = 16
Z = 160


def set_ends(entries, key, smallest, top_value):
    spot = [jax.random.randint(jax.random.fold_in(key, axis), (), 0, length) for axis, length in enumerate(entries.shape)]
    longest = entries.shape.index(max(entries.shape))
    beside = spot[:longest] + [(spot[longest] + 1) % entries.shape[longest]] + spot[longest + 1:]
    return entries.at[tuple(spot)].set(smallest).at[tuple(beside)].set(top_value)


def shard_levels(key, dims, cuts, low, largest):
    def one(axis_at, parts):
        draws = jax.random.uniform(jax.random.fold_in(jax.random.fold_in(key, 6), axis_at), (parts,), jnp.float32, low / len(cuts), largest / len(cuts))
        return jnp.repeat(jnp.exp(draws), dims[axis_at] // parts).reshape((-1,) + (1,) * (len(dims) - axis_at - 1))

    level = one(*cuts[0])
    for cut in cuts[1:]:
        level = level * one(*cut)
    return level


def gaussian(key, dims, spread, limit, shards=(), kind=jnp.bfloat16):
    values = jax.random.normal(key, dims, jnp.float32) * spread
    if len(shards) > 0:
        values = shard_levels(key, dims, shards, -0.22, 0.18) * values
    return jnp.clip(values, min=-limit, max=limit).astype(kind)


def setup_inputs(seed: int = 0) -> dict:
    keys = jax.random.split(jax.random.key(seed), 5)
    return {
        "images": gaussian(keys[0], (SUBJECTS, Z, X, Y), 1.0, 6.0, ((0, 16), (1, 32)), jnp.float32),
        "velocity": gaussian(keys[1], (3, SUBJECTS, Z, X, Y), 0.3, 3.0, ((1, 16), (2, 32)), jnp.float32),
        "ref_index": set_ends(jax.random.randint(keys[2], (NREF,), 0, SUBJECTS), jax.random.fold_in(keys[2], 1), 0, SUBJECTS - 1).astype(jnp.int32),
        "ref_weights": set_ends(jax.random.randint(keys[3], (SUBJECTS, NREF), 0, WDEN + 1), jax.random.fold_in(keys[3], 1), 0, WDEN).astype(jnp.int32),
    }


def gauss_taps():
    raw = [math.exp(-0.5 * offset * offset) for offset in range(-RG, RG + 1)]
    total = sum(raw)
    return [value / total for value in raw]


def window_sum(field, axis, taps):
    radius = len(taps) // 2
    widths = [(0, 0), (0, 0), (0, 0)]
    widths[axis] = (radius, radius)
    padded = jnp.pad(field, widths)
    length = field.shape[axis]
    total = taps[0] * lax.slice_in_dim(padded, 0, length, axis=axis)
    for offset in range(1, len(taps)):
        total = total + taps[offset] * lax.slice_in_dim(padded, offset, offset + length, axis=axis)
    return total


def filtered(field, taps):
    for axis in range(3):
        field = window_sum(field, axis, taps)
    return field


def boxed(field):
    return filtered(field, [1.0] * WIN) / float(WIN ** 3)


def central(field, axis):
    widths = [(0, 0), (0, 0), (0, 0)]
    widths[axis] = (1, 1)
    padded = jnp.pad(field, widths)
    length = field.shape[axis]
    upper = lax.slice_in_dim(padded, 2, length + 2, axis=axis)
    lower = lax.slice_in_dim(padded, 0, length, axis=axis)
    return (upper - lower) * 0.5


def reference(images, velocity, ref_index, ref_weights):
    taps = gauss_taps()

    def one_subject(inputs):
        moving, weights_row = inputs
        mean_i = boxed(moving)
        var_i = boxed(moving * moving) - mean_i * mean_i + 1e-5
        coeffs = jnp.zeros_like(moving)
        for refnum in range(NREF):
            fixed_img = images[ref_index[refnum]]
            mean_j = boxed(fixed_img)
            var_j = boxed(fixed_img * fixed_img) - mean_j * mean_j + 1e-5
            covariance = boxed(moving * fixed_img) - mean_i * mean_j
            term = 2.0 * covariance / (var_i * var_j) * ((fixed_img - mean_j) - covariance / var_i * (moving - mean_i))
            coeffs = coeffs + weights_row[refnum].astype(jnp.float32) / float(WDEN) * term
        return jnp.stack([filtered(coeffs * central(moving, axis), taps) for axis in range(3)])

    update = lax.map(one_subject, (images, ref_weights))
    return velocity + 40.0 * jnp.transpose(update, (1, 0, 2, 3, 4))
```

```python
import math

import jax
import jax.numpy as jnp
from jax import lax
from jax.experimental import pallas as pl
from jax.experimental.pallas import tpu as pltpu
from jax.sharding import PartitionSpec as P

X = 128
Y = 128
ZD = 5
NSUB = 16
NREF = 4
WIN = 9
RG = 3
WDEN = 16
RAD = WIN // 2
ROWS = X // NSUB
EXT_R = ROWS + 2 * RAD
EXT_P = ZD + 2 * RAD
CELLS = ROWS * ZD
NF = 2 + NREF
MESH = pl.DeviceIdType.MESH

XA, XB, ZA, ZB, CA0, CA1, CB0, CB1, IA, IB, FA, FB = range(12)


def gauss_taps():
    raw = [math.exp(-0.5 * offset * offset) for offset in range(-RG, RG + 1)]
    total = sum(raw)
    return [value / total for value in raw]


def chunk_of(s, hi):
    y, x = s // 4, s % 4
    ys = y + hi * (3 - 2 * y)
    return 4 * ys + x + (ys % 2) * (3 - 2 * x)


def subject_of(c, hi):
    ys, xs = c // 4, c % 4
    x = xs + (ys % 2) * (3 - 2 * xs)
    return 4 * (ys + hi * (3 - 2 * ys)) + x


def window_depth(v):
    core = ((v[4] + v[5]) + (v[6] + v[7])) + v[8]
    suf2 = v[2] + v[3]
    suf1 = v[1] + suf2
    suf0 = v[0] + suf1
    pre2 = v[9] + v[10]
    pre3 = pre2 + v[11]
    pre4 = pre3 + v[12]
    return [core + suf0, (core + suf1) + v[9], (core + suf2) + pre2, (core + v[3]) + pre3, core + pre4]


def window_rows(v):
    suf = [None] * 8
    pre = [None] * 8
    suf[7] = v[7]
    pre[0] = v[8]
    for i in range(6, -1, -1):
        suf[i] = v[i] + suf[i + 1]
    for i in range(1, 8):
        pre[i] = pre[i - 1] + v[8 + i]
    return [suf[i] + pre[i] for i in range(8)]


def band(taps, dtype):
    radius = len(taps) // 2
    diff = lax.broadcasted_iota(jnp.int32, (128, 128), 0) - lax.broadcasted_iota(jnp.int32, (128, 128), 1)
    matrix = jnp.zeros((128, 128), jnp.float32)
    for offset in range(len(taps)):
        matrix = jnp.where(diff == offset - radius, taps[offset], matrix)
    return matrix.astype(dtype)


def coeff_kernel(
    idx_ref, w_ref, img, cf, ih,
    a_buf, w_buf, ext, zs, xs, bx, inv, dev, c_buf, cs,
    sa, ra, sw, rw, sr, rr, sh, rh,
):
    s = lax.axis_index("subj")
    d = lax.axis_index("depth")
    nd = lax.axis_size("depth")
    half = nd // 2
    hi = d // half
    c = chunk_of(s, hi)
    mirror = 4 * (3 - s // 4) + s % 4
    has_lo, has_up = d > 0, d < nd - 1
    cross_lo, cross_up = d == half, d == half - 1
    s_lo = jnp.where(cross_lo, mirror, s)
    s_up = jnp.where(cross_up, mirror, s)

    barrier = pltpu.get_barrier_semaphore()
    for k in range(1, NSUB):
        pl.semaphore_signal(barrier, inc=1, device_id=((s + k) % NSUB, d), device_id_type=MESH)

    @pl.when(has_lo)
    def _():
        pl.semaphore_signal(barrier, inc=1, device_id=(s_lo, d - 1), device_id_type=MESH)

    @pl.when(has_up)
    def _():
        pl.semaphore_signal(barrier, inc=1, device_id=(s_up, d + 1), device_id_type=MESH)

    @pl.when(cross_lo)
    def _():
        pl.semaphore_signal(barrier, inc=1, device_id=(s, d - 1), device_id_type=MESH)

    @pl.when(cross_up)
    def _():
        pl.semaphore_signal(barrier, inc=1, device_id=(s, d + 1), device_id_type=MESH)

    rows = lax.broadcasted_iota(jnp.int32, (8, 128), 0)
    wt = jnp.zeros((8, 128), jnp.float32)
    for r in range(NREF):
        wt = jnp.where(rows == r, w_ref[0, r].astype(jnp.float32) * (1.0 / WDEN), wt)
    w_buf[s] = wt

    @pl.when(c == 0)
    def _():
        ext[0:RAD] = jnp.zeros((RAD, EXT_P, NSUB, Y), jnp.float32)

    @pl.when(c == NSUB - 1)
    def _():
        ext[RAD + ROWS:] = jnp.zeros((RAD, EXT_P, NSUB, Y), jnp.float32)

    @pl.when(jnp.logical_not(has_lo))
    def _():
        ext[:, 0:RAD] = jnp.zeros((EXT_R, RAD, NSUB, Y), jnp.float32)
        ih[0:4] = jnp.zeros((4, X, Y), jnp.float32)
        cf[0:RG] = jnp.zeros((RG, NSUB, ROWS, Y), jnp.float32)

    @pl.when(jnp.logical_not(has_up))
    def _():
        ext[:, RAD + ZD:] = jnp.zeros((EXT_R, RAD, NSUB, Y), jnp.float32)
        ih[4:8] = jnp.zeros((4, X, Y), jnp.float32)
        cf[RG + ZD:] = jnp.zeros((RG, NSUB, ROWS, Y), jnp.float32)

    extra = has_lo.astype(jnp.int32) + has_up.astype(jnp.int32) + cross_lo.astype(jnp.int32) + cross_up.astype(jnp.int32)
    pl.semaphore_wait(barrier, NSUB - 1 + extra)

    def remote(src, dst, send, recv, device):
        return pltpu.make_async_remote_copy(
            src_ref=src, dst_ref=dst, send_sem=send, recv_sem=recv, device_id=device, device_id_type=MESH
        )

    def chunk_out(k):
        to = (s + k) % NSUB
        return remote(img.at[:, chunk_of(to, hi)], a_buf.at[s], sa.at[k], ra.at[s], (to, d))

    def chunk_in(k):
        frm = (s + NSUB - k) % NSUB
        return remote(img.at[:, 0], a_buf.at[frm], sa.at[k], ra.at[frm], (frm, d))

    def weight_out(k):
        to = (s + k) % NSUB
        return remote(w_buf.at[s], w_buf.at[s], sw.at[k], rw.at[s], (to, d))

    def weight_in(k):
        frm = (s + NSUB - k) % NSUB
        return remote(w_buf.at[frm], w_buf.at[frm], sw.at[k], rw.at[frm], (frm, d))

    for k in range(1, NSUB):
        chunk_out(k).start()
    for k in range(1, NSUB):
        weight_out(k).start()
    a_buf[s] = img[:, c]
    for k in range(1, NSUB):
        chunk_in(k).wait_recv()

    a_flat = a_buf.reshape(NSUB * ZD * ROWS, Y)
    for p in range(ZD):
        for r in range(ROWS):
            ext[RAD + r, RAD + p] = a_flat[pl.ds(p * ROWS + r, NSUB, stride=ZD * ROWS), :]

    prev, nxt = subject_of(jnp.maximum(c - 1, 0), hi), subject_of(jnp.minimum(c + 1, NSUB - 1), hi)
    core_p = pl.ds(RAD, ZD)
    core_r = pl.ds(RAD, ROWS)
    last = RAD + ROWS
    x_dn = remote(ext.at[pl.ds(RAD, RAD), core_p], ext.at[pl.ds(last, RAD), core_p], sh.at[XA], rh.at[XA], (prev, d))
    x_up = remote(ext.at[pl.ds(ROWS, RAD), core_p], ext.at[pl.ds(0, RAD), core_p], sh.at[XB], rh.at[XB], (nxt, d))

    def z_dn(block, sem):
        return remote(ext.at[block, pl.ds(RAD, RAD)], ext.at[block, pl.ds(RAD + ZD, RAD)], sh.at[sem], rh.at[sem], (s_lo, d - 1))

    def z_up(block, sem):
        return remote(ext.at[block, pl.ds(ZD, RAD)], ext.at[block, pl.ds(0, RAD)], sh.at[sem], rh.at[sem], (s_up, d + 1))

    i_dn = remote(img.reshape(ZD, X, Y).at[pl.ds(0, 4)], ih.at[pl.ds(4, 4)], sh.at[IA], rh.at[IA], (s, d - 1))
    i_up = remote(img.reshape(ZD, X, Y).at[pl.ds(1, 4)], ih.at[pl.ds(0, 4)], sh.at[IB], rh.at[IB], (s, d + 1))
    has_prev, has_next = c > 0, c < NSUB - 1
    top, bottom = pl.ds(0, RAD), pl.ds(last, RAD)

    @pl.when(has_lo)
    def _():
        z_dn(core_r, ZA).start()

    @pl.when(has_up)
    def _():
        z_up(core_r, ZB).start()

    @pl.when(has_prev)
    def _():
        x_dn.start()

    @pl.when(has_next)
    def _():
        x_up.start()

    @pl.when(has_next)
    def _():
        x_dn.wait_recv()

        @pl.when(has_lo)
        def _():
            z_dn(bottom, CA1).start()

        @pl.when(has_up)
        def _():
            z_up(bottom, CB1).start()

    @pl.when(has_prev)
    def _():
        x_up.wait_recv()

        @pl.when(has_lo)
        def _():
            z_dn(top, CA0).start()

        @pl.when(has_up)
        def _():
            z_up(top, CB0).start()

    @pl.when(has_lo)
    def _():
        i_dn.start()

    @pl.when(has_up)
    def _():
        i_up.start()

    @pl.when(has_up)
    def _():
        z_dn(core_r, ZA).wait_recv()

        @pl.when(has_prev)
        def _():
            z_dn(top, CA0).wait_recv()

        @pl.when(has_next)
        def _():
            z_dn(bottom, CA1).wait_recv()

    @pl.when(has_lo)
    def _():
        z_up(core_r, ZB).wait_recv()

        @pl.when(has_prev)
        def _():
            z_up(top, CB0).wait_recv()

        @pl.when(has_next)
        def _():
            z_up(bottom, CB1).wait_recv()

    refs = [idx_ref[r] for r in range(NREF)]

    def depth_pass(row, carry):
        vals = [ext[row, p] for p in range(EXT_P)]
        for k, total in enumerate(window_depth(vals)):
            zs[0, row, k] = total
        for k, total in enumerate(window_depth([v * v for v in vals])):
            zs[1, row, k] = total
        for r in range(NREF):
            prods = [vals[p] * ext[row, p, pl.ds(refs[r], 1), :] for p in range(EXT_P)]
            for k, total in enumerate(window_depth(prods)):
                zs[2 + r, row, k] = total
        return carry

    lax.fori_loop(0, EXT_R, depth_pass, 0)

    def row_pass(f, carry):
        for k in range(ZD):
            for r, total in enumerate(window_rows([zs[f, row, k] for row in range(EXT_R)])):
                xs[f * CELLS + r * ZD + k] = total
        return carry

    lax.fori_loop(0, NF, row_pass, 0)

    ones = band([1.0] * WIN, jnp.bfloat16)
    ones2 = jnp.concatenate([ones, ones], axis=0)

    def lane_pass(b, carry):
        val = xs[pl.ds(b * 20, 20)].reshape(320, Y)
        high = val.astype(jnp.bfloat16)
        rest = val - high.astype(jnp.float32)
        mid = rest.astype(jnp.bfloat16)
        low = (rest - mid.astype(jnp.float32)).astype(jnp.bfloat16)
        total = jnp.dot(jnp.concatenate([high, mid], axis=1), ones2, preferred_element_type=jnp.float32)
        total = total + jnp.dot(low, ones, preferred_element_type=jnp.float32)
        bx[pl.ds(b * 20, 20)] = (total * (1.0 / WIN**3)).reshape(20, NSUB, Y)
        return carry

    lax.fori_loop(0, NF * CELLS // 20, lane_pass, 0)

    def stats(r, carry):
        for k in range(ZD):
            q = r * ZD + k
            mean = bx[q]
            inv[q] = 1.0 / (bx[CELLS + q] - mean * mean + 1e-5)
            dev[q] = ext[RAD + r, RAD + k] - mean
        return carry

    lax.fori_loop(0, ROWS, stats, 0)

    for k in range(1, NSUB):
        weight_in(k).wait_recv()
    w_flat = w_buf.reshape(NSUB * 8, 128)
    weights = [w_flat[pl.ds(r, NSUB, stride=8), :] for r in range(NREF)]

    def combine(row, carry):
        for k in range(ZD):
            q = row * ZD + k
            mean_i, inv_i, dev_i = bx[q], inv[q], dev[q]
            total = None
            for r in range(NREF):
                one = pl.ds(refs[r], 1)
                gain = (bx[(2 + r) * CELLS + q] - mean_i * bx[q, one, :]) * inv_i
                term = (2.0 * gain * inv[q, one, :]) * (dev[q, one, :] - gain * dev_i) * weights[r]
                total = term if total is None else total + term
            c_buf[pl.ds(q * NSUB, NSUB), :] = total
        return carry

    lax.fori_loop(0, ROWS, combine, 0)

    for sub in range(NSUB):
        for p in range(ZD):
            cs[sub, p] = c_buf[pl.ds(p * NSUB + sub, ROWS, stride=ZD * NSUB), :]

    planes = pl.ds(RG, ZD)

    def back_out(k):
        to = (s + k) % NSUB
        return remote(cs.at[to], cf.at[planes, c], sr.at[k], rr.at[c], (to, d))

    def back_in(k):
        frm = (s + NSUB - k) % NSUB
        chunk = chunk_of(frm, hi)
        return remote(cs.at[frm], cf.at[planes, chunk], sr.at[k], rr.at[chunk], (frm, d))

    for k in range(1, NSUB):
        back_out(k).start()
    cf[planes, c] = cs[s]
    for k in range(1, NSUB):
        back_in(k).wait_recv()

    f_dn = remote(cf.at[pl.ds(RG, RG)], cf.at[pl.ds(RG + ZD, RG)], sh.at[FA], rh.at[FA], (s, d - 1))
    f_up = remote(cf.at[pl.ds(ZD, RG)], cf.at[pl.ds(0, RG)], sh.at[FB], rh.at[FB], (s, d + 1))

    @pl.when(has_lo)
    def _():
        f_dn.start()

    @pl.when(has_up)
    def _():
        f_up.start()

    for k in range(1, NSUB):
        chunk_out(k).wait_send()
        weight_out(k).wait_send()
        back_out(k).wait_send()

    @pl.when(has_prev)
    def _():
        x_dn.wait_send()

    @pl.when(has_next)
    def _():
        x_up.wait_send()

    @pl.when(has_lo)
    def _():
        z_dn(core_r, ZA).wait_send()
        i_dn.wait_send()
        i_up.wait_recv()

        @pl.when(has_prev)
        def _():
            z_dn(top, CA0).wait_send()

        @pl.when(has_next)
        def _():
            z_dn(bottom, CA1).wait_send()

    @pl.when(has_up)
    def _():
        z_up(core_r, ZB).wait_send()
        i_up.wait_send()
        i_dn.wait_recv()

        @pl.when(has_prev)
        def _():
            z_up(top, CB0).wait_send()

        @pl.when(has_next)
        def _():
            z_up(bottom, CB1).wait_send()

    @pl.when(has_lo)
    def _():
        f_dn.wait_send()
        f_up.wait_recv()

    @pl.when(has_up)
    def _():
        f_up.wait_send()
        f_dn.wait_recv()


def smooth_kernel(cf, img, ih, vel, out, force):
    taps = gauss_taps()
    lane = lax.broadcasted_iota(jnp.int32, (X, Y), 1)
    row = lax.broadcasted_iota(jnp.int32, (X, Y), 0)

    def plane(i):
        if i < 4:
            return ih[i]
        if i < 4 + ZD:
            return img[i - 4]
        return ih[i - ZD]

    for p in range(ZD + 2 * RG):
        coef = cf[p] * 0.5
        here = plane(p + 1)
        force[0, p] = coef * (plane(p + 2) - plane(p))
        below = jnp.where(row == X - 1, 0.0, pltpu.roll(here, X - 1, 0))
        above = jnp.where(row == 0, 0.0, pltpu.roll(here, 1, 0))
        force[1, p] = coef * (below - above)
        after = jnp.where(lane == Y - 1, 0.0, pltpu.roll(here, Y - 1, 1))
        before = jnp.where(lane == 0, 0.0, pltpu.roll(here, 1, 1))
        force[2, p] = coef * (after - before)

    matrix = band(taps, jnp.float32)
    t_high = matrix.astype(jnp.bfloat16)
    t_low = (matrix - t_high.astype(jnp.float32)).astype(jnp.bfloat16)
    none = jnp.zeros((128, 128), jnp.bfloat16)
    right = jnp.concatenate(
        [jnp.concatenate([t_high, t_low], axis=1), jnp.concatenate([t_high, none], axis=1)], axis=0
    )
    left = jnp.concatenate(
        [jnp.concatenate([t_high, t_high], axis=1), jnp.concatenate([t_low, none], axis=1)], axis=0
    )

    def split(val):
        high = val.astype(jnp.bfloat16)
        return high, (val - high.astype(jnp.float32)).astype(jnp.bfloat16)

    def body(comp, carry):
        for p in range(ZD):
            total = taps[RG] * force[comp, p + RG]
            for k in range(1, RG + 1):
                total = total + taps[RG + k] * (force[comp, p + RG - k] + force[comp, p + RG + k])
            both = jnp.dot(jnp.concatenate(split(total), axis=1), right, preferred_element_type=jnp.float32)
            across = both[:, :Y] + both[:, Y:]
            both = jnp.dot(left, jnp.concatenate(split(across), axis=0), preferred_element_type=jnp.float32)
            out[comp, p] = vel[comp, p] + 40.0 * (both[:X] + both[X:])
        return carry

    lax.fori_loop(0, 3, body, 0)


def on_device(images, velocity, ref_index, ref_weights):
    vmem = pl.BlockSpec(memory_space=pltpu.VMEM)
    smem = pl.BlockSpec(memory_space=pltpu.SMEM)
    f32 = jnp.float32
    dma = pltpu.SemaphoreType.DMA
    cf, ih = pl.pallas_call(
        coeff_kernel,
        out_shape=(
            jax.ShapeDtypeStruct((ZD + 2 * RG, NSUB, ROWS, Y), f32),
            jax.ShapeDtypeStruct((8, X, Y), f32),
        ),
        in_specs=[smem, smem, vmem],
        out_specs=(vmem, vmem),
        scratch_shapes=[
            pltpu.VMEM((NSUB, ZD, ROWS, Y), f32),
            pltpu.VMEM((NSUB, 8, 128), f32),
            pltpu.VMEM((EXT_R, EXT_P, NSUB, Y), f32),
            pltpu.VMEM((NF, EXT_R, ZD, NSUB, Y), f32),
            pltpu.VMEM((NF * CELLS, NSUB, Y), f32),
            pltpu.VMEM((NF * CELLS, NSUB, Y), f32),
            pltpu.VMEM((CELLS, NSUB, Y), f32),
            pltpu.VMEM((CELLS, NSUB, Y), f32),
            pltpu.VMEM((CELLS * NSUB, Y), f32),
            pltpu.VMEM((NSUB, ZD, ROWS, Y), f32),
            dma((NSUB,)), dma((NSUB,)), dma((NSUB,)), dma((NSUB,)), dma((NSUB,)), dma((NSUB,)),
            dma((12,)), dma((12,)),
        ],
        compiler_params=pltpu.CompilerParams(
            collective_id=0, has_side_effects=True, vmem_limit_bytes=32 * 1024 * 1024
        ),
    )(ref_index, ref_weights, images.reshape(ZD, NSUB, ROWS, Y))
    out = pl.pallas_call(
        smooth_kernel,
        out_shape=jax.ShapeDtypeStruct((3, ZD, X, Y), f32),
        in_specs=[vmem] * 4,
        out_specs=vmem,
        scratch_shapes=[pltpu.VMEM((3, ZD + 2 * RG, X, Y), f32)],
        compiler_params=pltpu.CompilerParams(vmem_limit_bytes=32 * 1024 * 1024),
    )(cf.reshape(ZD + 2 * RG, X, Y), images.reshape(ZD, X, Y), ih, velocity.reshape(3, ZD, X, Y))
    return out.reshape(3, 1, ZD, X, Y)


def solution(mesh):
    placed = (
        P("subj", "depth", None, None),
        P(None, "subj", "depth", None, None),
        P(),
        P("subj", None),
    )
    return jax.shard_map(
        on_device,
        mesh=mesh,
        in_specs=placed,
        out_specs=P(None, "subj", "depth", None, None),
        check_vma=False,
    )
```

```python
import functools
import math

import jax
import jax.numpy as jnp
from jax import lax
from jax.experimental import pallas as pl
from jax.experimental.pallas import tpu as pltpu
from jax.sharding import PartitionSpec as P

X = 128
Y = 128
ZD = 5
NSUB = 16
NREF = 4
WIN = 9
RG = 3
WDEN = 16
RAD = WIN // 2
ROWS = X // NSUB
EXT_R = ROWS + 2 * RAD
EXT_P = ZD + 2 * RAD
CELLS = ROWS * ZD
NF = 2 + NREF
MESH = pl.DeviceIdType.MESH

XA, XB, ZA, ZB, CA0, CA1, CB0, CB1, IA, IB, FA, FB, YA, YB = range(14)


def gauss_taps():
    raw = [math.exp(-0.5 * offset * offset) for offset in range(-RG, RG + 1)]
    total = sum(raw)
    return [value / total for value in raw]


def chunk_of(s, hi):
    y, x = s // 4, s % 4
    ys = y + hi * (3 - 2 * y)
    return 4 * ys + x + (ys % 2) * (3 - 2 * x)


def subject_of(c, hi):
    ys, xs = c // 4, c % 4
    x = xs + (ys % 2) * (3 - 2 * xs)
    return 4 * (ys + hi * (3 - 2 * ys)) + x


def window_depth(v):
    core = ((v[4] + v[5]) + (v[6] + v[7])) + v[8]
    suf2 = v[2] + v[3]
    suf1 = v[1] + suf2
    suf0 = v[0] + suf1
    pre2 = v[9] + v[10]
    pre3 = pre2 + v[11]
    pre4 = pre3 + v[12]
    return [core + suf0, (core + suf1) + v[9], (core + suf2) + pre2, (core + v[3]) + pre3, core + pre4]


def window_rows(v):
    suf = [None] * 8
    pre = [None] * 8
    suf[7] = v[7]
    pre[0] = v[8]
    for i in range(6, -1, -1):
        suf[i] = v[i] + suf[i + 1]
    for i in range(1, 8):
        pre[i] = pre[i - 1] + v[8 + i]
    return [suf[i] + pre[i] for i in range(8)]


def band(taps, dtype):
    radius = len(taps) // 2
    diff = lax.broadcasted_iota(jnp.int32, (128, 128), 0) - lax.broadcasted_iota(jnp.int32, (128, 128), 1)
    matrix = jnp.zeros((128, 128), jnp.float32)
    for offset in range(len(taps)):
        matrix = jnp.where(diff == offset - radius, taps[offset], matrix)
    return matrix.astype(dtype)


def coeff_kernel(
    idx_ref, w_ref, img_hbm, cf, ih,
    img, a_buf, w_buf, ext, ext_top, ext_bot, zs, xs, bx, inv, dev, c_buf, cs, hs,
    sa, ra, sw, rw, sr, rr, sg, rg, sc, rc, sh, rh, load_sem,
):
    s = lax.axis_index("subj")
    d = lax.axis_index("depth")
    nd = lax.axis_size("depth")
    half = nd // 2
    hi = d // half
    c = chunk_of(s, hi)
    mirror = 4 * (3 - s // 4) + s % 4
    has_lo, has_up = d > 0, d < nd - 1
    cross_lo, cross_up = d == half, d == half - 1
    near_lo, near_up = has_lo & (d != half), has_up & (d != half - 1)
    has_prev, has_next = c > 0, c < NSUB - 1
    s_lo = jnp.where(cross_lo, mirror, s)
    s_up = jnp.where(cross_up, mirror, s)

    load = pltpu.make_async_copy(img_hbm, img, load_sem)
    load.start()

    barrier = pltpu.get_barrier_semaphore()
    for k in range(1, NSUB):
        pl.semaphore_signal(barrier, inc=1, device_id=((s + k) % NSUB, d), device_id_type=MESH)

    @pl.when(near_lo)
    def _():
        pl.semaphore_signal(barrier, inc=1, device_id=(s, d - 1), device_id_type=MESH)

    @pl.when(near_up)
    def _():
        pl.semaphore_signal(barrier, inc=1, device_id=(s, d + 1), device_id_type=MESH)

    @pl.when(cross_lo)
    def _():
        for k in range(NSUB):
            pl.semaphore_signal(barrier, inc=1, device_id=((s + k) % NSUB, d - 1), device_id_type=MESH)

    @pl.when(cross_up)
    def _():
        for k in range(NSUB):
            pl.semaphore_signal(barrier, inc=1, device_id=((s + k) % NSUB, d + 1), device_id_type=MESH)

    rows = lax.broadcasted_iota(jnp.int32, (8, 128), 0)
    wt = jnp.zeros((8, 128), jnp.float32)
    for r in range(NREF):
        wt = jnp.where(rows == r, w_ref[0, r].astype(jnp.float32) * (1.0 / WDEN), wt)
    w_buf[s] = wt

    @pl.when(c == 0)
    def _():
        ext_top[...] = jnp.zeros((RAD, EXT_P, NSUB, Y), jnp.float32)

    @pl.when(c == NSUB - 1)
    def _():
        ext_bot[...] = jnp.zeros((RAD, EXT_P, NSUB, Y), jnp.float32)

    @pl.when(jnp.logical_not(has_lo))
    def _():
        ext[:, 0:RAD] = jnp.zeros((ROWS, RAD, NSUB, Y), jnp.float32)
        ext_top[:, 0:RAD] = jnp.zeros((RAD, RAD, NSUB, Y), jnp.float32)
        ext_bot[:, 0:RAD] = jnp.zeros((RAD, RAD, NSUB, Y), jnp.float32)
        ih[0:4] = jnp.zeros((4, NSUB, ROWS, Y), jnp.float32)
        cf[0:RG] = jnp.zeros((RG, NSUB, ROWS, Y), jnp.float32)

    @pl.when(jnp.logical_not(has_up))
    def _():
        ext[:, RAD + ZD:] = jnp.zeros((ROWS, RAD, NSUB, Y), jnp.float32)
        ext_top[:, RAD + ZD:] = jnp.zeros((RAD, RAD, NSUB, Y), jnp.float32)
        ext_bot[:, RAD + ZD:] = jnp.zeros((RAD, RAD, NSUB, Y), jnp.float32)
        ih[4:8] = jnp.zeros((4, NSUB, ROWS, Y), jnp.float32)
        cf[RG + ZD:] = jnp.zeros((RG, NSUB, ROWS, Y), jnp.float32)

    load.wait()
    one_if = lambda cond: cond.astype(jnp.int32)
    extra = one_if(near_lo) + one_if(near_up) + NSUB * (one_if(cross_lo) + one_if(cross_up))
    pl.semaphore_wait(barrier, NSUB - 1 + extra)

    def remote(src, dst, send, recv, device):
        return pltpu.make_async_remote_copy(
            src_ref=src, dst_ref=dst, send_sem=send, recv_sem=recv, device_id=device, device_id_type=MESH
        )

    def peer_to(k):
        return (s + k) % NSUB

    def peer_from(k):
        return (s + NSUB - k) % NSUB

    def chunk_out(k):
        to = peer_to(k)
        return remote(img.at[:, chunk_of(to, hi)], a_buf.at[s], sa.at[k], ra.at[s], (to, d))

    def chunk_in(k):
        frm = peer_from(k)
        return remote(img.at[:, 0], a_buf.at[frm], sa.at[k], ra.at[frm], (frm, d))

    def weight_out(k):
        return remote(w_buf.at[s], w_buf.at[s], sw.at[k], rw.at[s], (peer_to(k), d))

    def weight_in(k):
        frm = peer_from(k)
        return remote(w_buf.at[frm], w_buf.at[frm], sw.at[k], rw.at[frm], (frm, d))

    def spread():
        for k in range(1, NSUB):
            chunk_out(k).start()
        for k in range(1, NSUB):
            weight_out(k).start()
        a_buf[s] = img[:, c]
        for k in range(1, NSUB):
            chunk_in(k).wait_recv()
        a_flat = a_buf.reshape(NSUB * ZD * ROWS, Y)
        for p in range(ZD):
            for r in range(ROWS):
                ext[r, RAD + p] = a_flat[pl.ds(p * ROWS + r, NSUB, stride=ZD * ROWS), :]

    prev, nxt = subject_of(jnp.maximum(c - 1, 0), hi), subject_of(jnp.minimum(c + 1, NSUB - 1), hi)
    core_p = pl.ds(RAD, ZD)
    low_p, high_p = pl.ds(0, RAD), pl.ds(RAD + ZD, RAD)

    def x_dn(planes, send, recv):
        return remote(ext.at[pl.ds(0, RAD), planes], ext_bot.at[:, planes], sh.at[send], rh.at[recv], (prev, d))

    def x_up(planes, send, recv):
        return remote(ext.at[pl.ds(RAD, RAD), planes], ext_top.at[:, planes], sh.at[send], rh.at[recv], (nxt, d))

    def z_dn(block, sem):
        return remote(block.at[:, pl.ds(RAD, RAD)], block.at[:, high_p], sh.at[sem], rh.at[sem], (s_lo, d - 1))

    def z_up(block, sem):
        return remote(block.at[:, pl.ds(ZD, RAD)], block.at[:, low_p], sh.at[sem], rh.at[sem], (s_up, d + 1))

    def i_dn():
        return remote(img.at[pl.ds(0, 4)], ih.at[pl.ds(4, 4)], sh.at[IA], rh.at[IA], (s, d - 1))

    def i_up():
        return remote(img.at[pl.ds(1, 4)], ih.at[pl.ds(0, 4)], sh.at[IB], rh.at[IB], (s, d + 1))

    def across_dn_x(go):
        @pl.when(has_prev)
        def _():
            @pl.when(cross_up)
            def _():
                go(x_dn(high_p, YA, CA1))

            @pl.when(cross_lo)
            def _():
                go(x_dn(low_p, YA, CB1))

    def across_up_x(go):
        @pl.when(has_next)
        def _():
            @pl.when(cross_up)
            def _():
                go(x_up(high_p, YB, CA0))

            @pl.when(cross_lo)
            def _():
                go(x_up(low_p, YB, CB0))

    def halo_start():
        @pl.when(has_lo)
        def _():
            z_dn(ext, ZA).start()

        @pl.when(has_up)
        def _():
            z_up(ext, ZB).start()

        @pl.when(has_prev)
        def _():
            x_dn(core_p, XA, XA).start()

        @pl.when(has_next)
        def _():
            x_up(core_p, XB, XB).start()

        @pl.when(has_next)
        def _():
            x_dn(core_p, XA, XA).wait_recv()

            @pl.when(near_lo)
            def _():
                z_dn(ext_bot, CA1).start()

            @pl.when(near_up)
            def _():
                z_up(ext_bot, CB1).start()

        @pl.when(has_prev)
        def _():
            x_up(core_p, XB, XB).wait_recv()

            @pl.when(near_lo)
            def _():
                z_dn(ext_top, CA0).start()

            @pl.when(near_up)
            def _():
                z_up(ext_top, CB0).start()

        @pl.when(has_up)
        def _():
            z_dn(ext, ZA).wait_recv()

        @pl.when(has_lo)
        def _():
            z_up(ext, ZB).wait_recv()

        across_dn_x(lambda copy: copy.start())
        across_up_x(lambda copy: copy.start())

        @pl.when(near_lo)
        def _():
            i_dn().start()

        @pl.when(near_up)
        def _():
            i_up().start()

    e_flat = ext.reshape(ROWS * EXT_P * NSUB, Y)

    def slab_out(k, first):
        to = peer_to(k)
        return remote(hs.at[to], ih.at[pl.ds(first, 4), c], sg.at[k], rg.at[c], (to, d))

    def slab_in(k, first):
        frm = peer_from(k)
        chunk = chunk_of(frm, hi)
        return remote(hs.at[frm], ih.at[pl.ds(first, 4), chunk], sg.at[k], rg.at[chunk], (frm, d))

    def slab_start(base, first):
        for sub in range(NSUB):
            for p in range(4):
                at = (base + p) * NSUB + sub
                hs[sub, p] = e_flat[pl.ds(at, ROWS, stride=EXT_P * NSUB), :]
        for k in range(1, NSUB):
            slab_out(k, first).start()
        ih[pl.ds(first, 4), c] = hs[s]

    def slabs():
        @pl.when(cross_lo)
        def _():
            slab_start(0, 0)

        @pl.when(cross_up)
        def _():
            slab_start(RAD + ZD, 4)

    def corners_end():
        @pl.when(has_up)
        def _():
            @pl.when(has_prev)
            def _():
                z_dn(ext_top, CA0).wait_recv()

            @pl.when(has_next)
            def _():
                z_dn(ext_bot, CA1).wait_recv()

        @pl.when(has_lo)
        def _():
            @pl.when(has_prev)
            def _():
                z_up(ext_top, CB0).wait_recv()

            @pl.when(has_next)
            def _():
                z_up(ext_bot, CB1).wait_recv()

    refs = [idx_ref[r] for r in range(NREF)]

    def depth_pass(block, first, row, carry):
        at = row + first
        vals = [block[row, p] for p in range(EXT_P)]
        for k, total in enumerate(window_depth(vals)):
            zs[0, at, k] = total
        for k, total in enumerate(window_depth([v * v for v in vals])):
            zs[1, at, k] = total
        for r in range(NREF):
            prods = [vals[p] * block[row, p, pl.ds(refs[r], 1), :] for p in range(EXT_P)]
            for k, total in enumerate(window_depth(prods)):
                zs[2 + r, at, k] = total
        return carry

    def row_pass(f, carry):
        for k in range(ZD):
            for r, total in enumerate(window_rows([zs[f, row, k] for row in range(EXT_R)])):
                xs[f * CELLS + r * ZD + k] = total
        return carry

    def core_rows():
        lax.fori_loop(0, ROWS, functools.partial(depth_pass, ext, RAD), 0)

    def other_rows():
        lax.fori_loop(0, RAD, functools.partial(depth_pass, ext_top, 0), 0)
        lax.fori_loop(0, RAD, functools.partial(depth_pass, ext_bot, RAD + ROWS), 0)

    def boxes():
        lax.fori_loop(0, NF, row_pass, 0)
        ones = band([1.0] * WIN, jnp.bfloat16)
        ones2 = jnp.concatenate([ones, ones], axis=0)

        def lane_pass(b, carry):
            val = xs[pl.ds(b * 20, 20)].reshape(320, Y)
            high = val.astype(jnp.bfloat16)
            rest = val - high.astype(jnp.float32)
            mid = rest.astype(jnp.bfloat16)
            low = (rest - mid.astype(jnp.float32)).astype(jnp.bfloat16)
            total = jnp.dot(jnp.concatenate([high, mid], axis=1), ones2, preferred_element_type=jnp.float32)
            total = total + jnp.dot(low, ones, preferred_element_type=jnp.float32)
            bx[pl.ds(b * 20, 20)] = (total * (1.0 / WIN**3)).reshape(20, NSUB, Y)
            return carry

        lax.fori_loop(0, NF * CELLS // 20, lane_pass, 0)

    def combined():
        def stats(r, carry):
            for k in range(ZD):
                q = r * ZD + k
                mean = bx[q]
                inv[q] = 1.0 / (bx[CELLS + q] - mean * mean + 1e-5)
                dev[q] = ext[r, RAD + k] - mean
            return carry

        lax.fori_loop(0, ROWS, stats, 0)
        for k in range(1, NSUB):
            weight_in(k).wait_recv()
        w_flat = w_buf.reshape(NSUB * 8, 128)
        weights = [w_flat[pl.ds(r, NSUB, stride=8), :] for r in range(NREF)]

        def combine(row, carry):
            for k in range(ZD):
                q = row * ZD + k
                mean_i, inv_i, dev_i = bx[q], inv[q], dev[q]
                total = None
                for r in range(NREF):
                    one = pl.ds(refs[r], 1)
                    gain = (bx[(2 + r) * CELLS + q] - mean_i * bx[q, one, :]) * inv_i
                    term = (2.0 * gain * inv[q, one, :]) * (dev[q, one, :] - gain * dev_i) * weights[r]
                    total = term if total is None else total + term
                c_buf[pl.ds(q * NSUB, NSUB), :] = total
            return carry

        lax.fori_loop(0, ROWS, combine, 0)
        for sub in range(NSUB):
            for p in range(ZD):
                cs[sub, p] = c_buf[pl.ds(p * NSUB + sub, ROWS, stride=ZD * NSUB), :]

    planes = pl.ds(RG, ZD)

    def back_out(k):
        to = peer_to(k)
        return remote(cs.at[to], cf.at[planes, c], sr.at[k], rr.at[c], (to, d))

    def back_in(k):
        frm = peer_from(k)
        chunk = chunk_of(frm, hi)
        return remote(cs.at[frm], cf.at[planes, chunk], sr.at[k], rr.at[chunk], (frm, d))

    def over_up(k):
        to = peer_to(k)
        return remote(cs.at[to, pl.ds(2, RG)], cf.at[pl.ds(0, RG), c], sc.at[k], rc.at[c], (to, d + 1))

    def over_dn(k):
        to = peer_to(k)
        return remote(cs.at[to, pl.ds(0, RG)], cf.at[pl.ds(RG + ZD, RG), c], sc.at[k], rc.at[c], (to, d - 1))

    def over_in(k, first, side):
        return remote(cs.at[k, pl.ds(0, RG)], cf.at[pl.ds(first, RG), k], sc.at[k], rc.at[k], (s, side))

    def f_dn():
        return remote(cf.at[pl.ds(RG, RG)], cf.at[pl.ds(RG + ZD, RG)], sh.at[FA], rh.at[FA], (s, d - 1))

    def f_up():
        return remote(cf.at[pl.ds(ZD, RG)], cf.at[pl.ds(0, RG)], sh.at[FB], rh.at[FB], (s, d + 1))

    def home():
        @pl.when(cross_up)
        def _():
            for k in range(NSUB):
                over_up(k).start()

        @pl.when(cross_lo)
        def _():
            for k in range(NSUB):
                over_dn(k).start()

        for k in range(1, NSUB):
            back_out(k).start()
        cf[planes, c] = cs[s]
        for k in range(1, NSUB):
            back_in(k).wait_recv()

        @pl.when(near_lo)
        def _():
            f_dn().start()

        @pl.when(near_up)
        def _():
            f_up().start()

    def halo_drain():
        @pl.when(has_prev)
        def _():
            x_dn(core_p, XA, XA).wait_send()

        @pl.when(has_next)
        def _():
            x_up(core_p, XB, XB).wait_send()

        across_dn_x(lambda copy: copy.wait_send())
        across_up_x(lambda copy: copy.wait_send())

        @pl.when(has_lo)
        def _():
            z_dn(ext, ZA).wait_send()

        @pl.when(has_up)
        def _():
            z_up(ext, ZB).wait_send()

        @pl.when(near_lo)
        def _():
            i_dn().wait_send()
            i_up().wait_recv()

            @pl.when(has_prev)
            def _():
                z_dn(ext_top, CA0).wait_send()

            @pl.when(has_next)
            def _():
                z_dn(ext_bot, CA1).wait_send()

        @pl.when(near_up)
        def _():
            i_up().wait_send()
            i_dn().wait_recv()

            @pl.when(has_prev)
            def _():
                z_up(ext_top, CB0).wait_send()

            @pl.when(has_next)
            def _():
                z_up(ext_bot, CB1).wait_send()

    def slab_drain():
        def both(first):
            for k in range(1, NSUB):
                slab_out(k, first).wait_send()
                slab_in(k, first).wait_recv()

        @pl.when(cross_lo)
        def _():
            both(0)

        @pl.when(cross_up)
        def _():
            both(4)

    def spread_drain():
        for k in range(1, NSUB):
            chunk_out(k).wait_send()
            weight_out(k).wait_send()

    def home_drain():
        for k in range(1, NSUB):
            back_out(k).wait_send()

        @pl.when(cross_up)
        def _():
            for k in range(NSUB):
                over_up(k).wait_send()
                over_in(k, RG + ZD, d + 1).wait_recv()

        @pl.when(cross_lo)
        def _():
            for k in range(NSUB):
                over_dn(k).wait_send()
                over_in(k, 0, d - 1).wait_recv()

        @pl.when(near_lo)
        def _():
            f_dn().wait_send()
            f_up().wait_recv()

        @pl.when(near_up)
        def _():
            f_up().wait_send()
            f_dn().wait_recv()

    spread()
    halo_start()
    slabs()
    core_rows()
    corners_end()
    other_rows()
    boxes()
    combined()
    home()
    spread_drain()
    halo_drain()
    slab_drain()
    home_drain()


def smooth_kernel(cf, img, ih, vel, out, force):
    taps = gauss_taps()
    lane = lax.broadcasted_iota(jnp.int32, (X, Y), 1)
    row = lax.broadcasted_iota(jnp.int32, (X, Y), 0)
    comp = pl.program_id(0)

    def plane(i):
        if i < 4:
            return ih[i]
        if i < 4 + ZD:
            return img[i - 4]
        return ih[i - ZD]

    @pl.when(comp == 0)
    def _():
        for p in range(ZD + 2 * RG):
            force[p] = (cf[p] * 0.5) * (plane(p + 2) - plane(p))

    @pl.when(comp == 1)
    def _():
        for p in range(ZD + 2 * RG):
            here = plane(p + 1)
            below = jnp.where(row == X - 1, 0.0, pltpu.roll(here, X - 1, 0))
            above = jnp.where(row == 0, 0.0, pltpu.roll(here, 1, 0))
            force[p] = (cf[p] * 0.5) * (below - above)

    @pl.when(comp == 2)
    def _():
        for p in range(ZD + 2 * RG):
            here = plane(p + 1)
            after = jnp.where(lane == Y - 1, 0.0, pltpu.roll(here, Y - 1, 1))
            before = jnp.where(lane == 0, 0.0, pltpu.roll(here, 1, 1))
            force[p] = (cf[p] * 0.5) * (after - before)

    matrix = band(taps, jnp.float32)
    t_high = matrix.astype(jnp.bfloat16)
    t_low = (matrix - t_high.astype(jnp.float32)).astype(jnp.bfloat16)
    none = jnp.zeros((128, 128), jnp.bfloat16)
    right = jnp.concatenate(
        [jnp.concatenate([t_high, t_low], axis=1), jnp.concatenate([t_high, none], axis=1)], axis=0
    )
    left = jnp.concatenate(
        [jnp.concatenate([t_high, t_high], axis=1), jnp.concatenate([t_low, none], axis=1)], axis=0
    )

    def split(val):
        high = val.astype(jnp.bfloat16)
        return high, (val - high.astype(jnp.float32)).astype(jnp.bfloat16)

    for p in range(ZD):
        total = taps[RG] * force[p + RG]
        for k in range(1, RG + 1):
            total = total + taps[RG + k] * (force[p + RG - k] + force[p + RG + k])
        both = jnp.dot(jnp.concatenate(split(total), axis=1), right, preferred_element_type=jnp.float32)
        across = both[:, :Y] + both[:, Y:]
        both = jnp.dot(left, jnp.concatenate(split(across), axis=0), preferred_element_type=jnp.float32)
        out[0, p] = vel[0, p] + 40.0 * (both[:X] + both[X:])


def on_device(images, velocity, ref_index, ref_weights):
    vmem = pl.BlockSpec(memory_space=pltpu.VMEM)
    smem = pl.BlockSpec(memory_space=pltpu.SMEM)
    f32 = jnp.float32
    dma = pltpu.SemaphoreType.DMA
    cf, ih = pl.pallas_call(
        coeff_kernel,
        out_shape=(
            jax.ShapeDtypeStruct((ZD + 2 * RG, NSUB, ROWS, Y), f32),
            jax.ShapeDtypeStruct((8, NSUB, ROWS, Y), f32),
        ),
        in_specs=[smem, smem, pl.BlockSpec(memory_space=pltpu.HBM)],
        out_specs=(vmem, vmem),
        scratch_shapes=[
            pltpu.VMEM((ZD, NSUB, ROWS, Y), f32),
            pltpu.VMEM((NSUB, ZD, ROWS, Y), f32),
            pltpu.VMEM((NSUB, 8, 128), f32),
            pltpu.VMEM((ROWS, EXT_P, NSUB, Y), f32),
            pltpu.VMEM((RAD, EXT_P, NSUB, Y), f32),
            pltpu.VMEM((RAD, EXT_P, NSUB, Y), f32),
            pltpu.VMEM((NF, EXT_R, ZD, NSUB, Y), f32),
            pltpu.VMEM((NF * CELLS, NSUB, Y), f32),
            pltpu.VMEM((NF * CELLS, NSUB, Y), f32),
            pltpu.VMEM((CELLS, NSUB, Y), f32),
            pltpu.VMEM((CELLS, NSUB, Y), f32),
            pltpu.VMEM((CELLS * NSUB, Y), f32),
            pltpu.VMEM((NSUB, ZD, ROWS, Y), f32),
            pltpu.VMEM((NSUB, 4, ROWS, Y), f32),
            dma((NSUB,)), dma((NSUB,)), dma((NSUB,)), dma((NSUB,)), dma((NSUB,)),
            dma((NSUB,)), dma((NSUB,)), dma((NSUB,)), dma((NSUB,)), dma((NSUB,)),
            dma((14,)), dma((14,)), dma,
        ],
        compiler_params=pltpu.CompilerParams(
            collective_id=0, has_side_effects=True, vmem_limit_bytes=32 * 1024 * 1024
        ),
    )(ref_index, ref_weights, images.reshape(ZD, NSUB, ROWS, Y))
    out = pl.pallas_call(
        smooth_kernel,
        out_shape=jax.ShapeDtypeStruct((3, ZD, X, Y), f32),
        grid=(3,),
        in_specs=[vmem] * 3 + [pl.BlockSpec((1, ZD, X, Y), lambda i: (i, 0, 0, 0))],
        out_specs=pl.BlockSpec((1, ZD, X, Y), lambda i: (i, 0, 0, 0)),
        scratch_shapes=[pltpu.VMEM((ZD + 2 * RG, X, Y), f32)],
        compiler_params=pltpu.CompilerParams(vmem_limit_bytes=32 * 1024 * 1024),
    )(cf.reshape(ZD + 2 * RG, X, Y), images.reshape(ZD, X, Y), ih.reshape(8, X, Y), velocity.reshape(3, ZD, X, Y))
    return out.reshape(3, 1, ZD, X, Y)


def solution(mesh):
    placed = (
        P("subj", "depth", None, None),
        P(None, "subj", "depth", None, None),
        P(),
        P("subj", None),
    )
    return jax.shard_map(
        on_device,
        mesh=mesh,
        in_specs=placed,
        out_specs=P(None, "subj", "depth", None, None),
        check_vma=False,
    )
```

```python
import functools
import math

import jax
import jax.numpy as jnp
from jax import lax
from jax.experimental import pallas as pl
from jax.experimental.pallas import tpu as pltpu
from jax.sharding import PartitionSpec as P

X = 128
Y = 128
ZD = 5
NSUB = 16
NREF = 4
WIN = 9
RG = 3
WDEN = 16
RAD = WIN // 2
ROWS = X // NSUB
EXT_R = ROWS + 2 * RAD
EXT_P = ZD + 2 * RAD
CELLS = ROWS * ZD
NF = 2 + NREF
FP = ZD + 2 * RG
VLIM = 32
MESH = pl.DeviceIdType.MESH

XA, XB, ZA, ZB, CA0, CA1, CB0, CB1, IA, IB, YA, YB, FA, FB = list(range(13)) + [16]


def gauss_taps():
    raw = [math.exp(-0.5 * offset * offset) for offset in range(-RG, RG + 1)]
    total = sum(raw)
    return [value / total for value in raw]


def chunk_of(s, hi):
    y, x = s // 4, s % 4
    ys = y + hi * (3 - 2 * y)
    return 4 * ys + x + (ys % 2) * (3 - 2 * x)


def subject_of(c, hi):
    ys, xs = c // 4, c % 4
    x = xs + (ys % 2) * (3 - 2 * xs)
    return 4 * (ys + hi * (3 - 2 * ys)) + x


def window_depth(v):
    core = ((v[4] + v[5]) + (v[6] + v[7])) + v[8]
    suf2 = v[2] + v[3]
    suf1 = v[1] + suf2
    suf0 = v[0] + suf1
    pre2 = v[9] + v[10]
    pre3 = pre2 + v[11]
    pre4 = pre3 + v[12]
    return [core + suf0, (core + suf1) + v[9], (core + suf2) + pre2, (core + v[3]) + pre3, core + pre4]


def window_rows(v):
    suf = [None] * 8
    pre = [None] * 8
    suf[7] = v[7]
    pre[0] = v[8]
    for i in range(6, -1, -1):
        suf[i] = v[i] + suf[i + 1]
    for i in range(1, 8):
        pre[i] = pre[i - 1] + v[8 + i]
    return [suf[i] + pre[i] for i in range(8)]


def band(taps, dtype):
    radius = len(taps) // 2
    diff = lax.broadcasted_iota(jnp.int32, (128, 128), 0) - lax.broadcasted_iota(jnp.int32, (128, 128), 1)
    matrix = jnp.zeros((128, 128), jnp.float32)
    for offset in range(len(taps)):
        matrix = jnp.where(diff == offset - radius, taps[offset], matrix)
    return matrix.astype(dtype)


def coeff_kernel(
    idx_ref, w_ref, img_hbm, out,
    img, a_buf, w_buf, ext, ext_top, ext_bot, zs, xs, bx, inv, dev, c_buf, cs, b_buf, cf, ih, grad, part,
    sa, ra, sw, rw, sr, rr, sb, rb, sg, rg, sc, rc, sh, rh, load_sem,
):
    s = lax.axis_index("subj")
    d = lax.axis_index("depth")
    nd = lax.axis_size("depth")
    half = nd // 2
    hi = d // half
    c = chunk_of(s, hi)
    has_lo, has_up = d > 0, d < nd - 1
    cross_lo, cross_up = d == half, d == half - 1
    near_lo, near_up = has_lo & (d != half), has_up & (d != half - 1)
    has_prev, has_next = c > 0, c < NSUB - 1
    load = pltpu.make_async_copy(img_hbm, img, load_sem)
    load.start()

    barrier = pltpu.get_barrier_semaphore()
    for k in range(1, NSUB):
        pl.semaphore_signal(barrier, inc=1, device_id=((s + k) % NSUB, d), device_id_type=MESH)

    @pl.when(near_lo)
    def _():
        pl.semaphore_signal(barrier, inc=1, device_id=(s, d - 1), device_id_type=MESH)

    @pl.when(near_up)
    def _():
        pl.semaphore_signal(barrier, inc=1, device_id=(s, d + 1), device_id_type=MESH)

    @pl.when(cross_lo)
    def _():
        for k in range(NSUB):
            pl.semaphore_signal(barrier, inc=1, device_id=((s + k) % NSUB, d - 1), device_id_type=MESH)

    @pl.when(cross_up)
    def _():
        for k in range(NSUB):
            pl.semaphore_signal(barrier, inc=1, device_id=((s + k) % NSUB, d + 1), device_id_type=MESH)

    rows = lax.broadcasted_iota(jnp.int32, (8, 128), 0)
    wt = jnp.zeros((8, 128), jnp.float32)
    for r in range(NREF):
        wt = jnp.where(rows == r, w_ref[0, r].astype(jnp.float32) * (1.0 / WDEN), wt)
    w_buf[s] = wt

    @pl.when(c == 0)
    def _():
        ext_top[...] = jnp.zeros((RAD, EXT_P, NSUB, Y), jnp.float32)

    @pl.when(c == NSUB - 1)
    def _():
        ext_bot[...] = jnp.zeros((RAD, EXT_P, NSUB, Y), jnp.float32)

    @pl.when(jnp.logical_not(has_lo))
    def _():
        ext[:, 0:RAD] = jnp.zeros((ROWS, RAD, NSUB, Y), jnp.float32)
        ext_top[:, 0:RAD] = jnp.zeros((RAD, RAD, NSUB, Y), jnp.float32)
        ext_bot[:, 0:RAD] = jnp.zeros((RAD, RAD, NSUB, Y), jnp.float32)
        ih[0:4] = jnp.zeros((4, NSUB, ROWS, Y), jnp.float32)
        cf[0:RG] = jnp.zeros((RG, NSUB, ROWS, Y), jnp.float32)

    @pl.when(jnp.logical_not(has_up))
    def _():
        ext[:, RAD + ZD:] = jnp.zeros((ROWS, RAD, NSUB, Y), jnp.float32)
        ext_top[:, RAD + ZD:] = jnp.zeros((RAD, RAD, NSUB, Y), jnp.float32)
        ext_bot[:, RAD + ZD:] = jnp.zeros((RAD, RAD, NSUB, Y), jnp.float32)
        ih[4:8] = jnp.zeros((4, NSUB, ROWS, Y), jnp.float32)
        cf[RG + ZD:] = jnp.zeros((RG, NSUB, ROWS, Y), jnp.float32)

    load.wait()
    one_if = lambda cond: cond.astype(jnp.int32)
    extra = one_if(near_lo) + one_if(near_up) + NSUB * (one_if(cross_lo) + one_if(cross_up))
    pl.semaphore_wait(barrier, NSUB - 1 + extra)

    def remote(src, dst, send, recv, device):
        return pltpu.make_async_remote_copy(
            src_ref=src, dst_ref=dst, send_sem=send, recv_sem=recv, device_id=device, device_id_type=MESH
        )

    def peer_to(k):
        return (s + k) % NSUB

    def peer_from(k):
        return (s + NSUB - k) % NSUB

    def chunk_out(k):
        to = peer_to(k)
        return remote(img.at[:, chunk_of(to, hi)], a_buf.at[s], sa.at[k], ra.at[s], (to, d))

    def chunk_in(k):
        frm = peer_from(k)
        return remote(img.at[:, 0], a_buf.at[frm], sa.at[k], ra.at[frm], (frm, d))

    def weight_out(k):
        return remote(w_buf.at[s], w_buf.at[s], sw.at[k], rw.at[s], (peer_to(k), d))

    def weight_in(k):
        frm = peer_from(k)
        return remote(w_buf.at[frm], w_buf.at[frm], sw.at[k], rw.at[frm], (frm, d))

    def far_out(k, first, side):
        to = peer_to(k)
        return remote(img.at[pl.ds(first, 4), chunk_of(to, 1 - hi)], b_buf.at[s], sb.at[k], rb.at[s], (to, side))

    def far_in(k, side):
        return remote(b_buf.at[k], b_buf.at[k], sb.at[k], rb.at[k], (s, side))

    def spread():
        for k in range(1, NSUB):
            chunk_out(k).start()

        @pl.when(cross_up)
        def _():
            for k in range(NSUB):
                far_out(k, 1, d + 1).start()

        @pl.when(cross_lo)
        def _():
            for k in range(NSUB):
                far_out(k, 0, d - 1).start()

        a_buf[s] = img[:, c]
        for k in range(1, NSUB):
            chunk_in(k).wait_recv()
        a_flat = a_buf.reshape(NSUB * ZD * ROWS, Y)
        for p in range(ZD):
            for r in range(ROWS):
                ext[r, RAD + p] = a_flat[pl.ds(p * ROWS + r, NSUB, stride=ZD * ROWS), :]

    prev, nxt = subject_of(jnp.maximum(c - 1, 0), hi), subject_of(jnp.minimum(c + 1, NSUB - 1), hi)
    core_p = pl.ds(RAD, ZD)
    low_p, high_p = pl.ds(0, RAD), pl.ds(RAD + ZD, RAD)

    def x_dn(planes, send, recv):
        return remote(ext.at[pl.ds(0, RAD), planes], ext_bot.at[:, planes], sh.at[send], rh.at[recv], (prev, d))

    def x_up(planes, send, recv):
        return remote(ext.at[pl.ds(RAD, RAD), planes], ext_top.at[:, planes], sh.at[send], rh.at[recv], (nxt, d))

    def z_dn(block, sem):
        return remote(block.at[:, pl.ds(RAD, RAD)], block.at[:, high_p], sh.at[sem], rh.at[sem], (s, d - 1))

    def z_up(block, sem):
        return remote(block.at[:, pl.ds(ZD, RAD)], block.at[:, low_p], sh.at[sem], rh.at[sem], (s, d + 1))

    def i_dn():
        return remote(img.at[pl.ds(0, 4)], ih.at[pl.ds(4, 4)], sh.at[IA], rh.at[IA], (s, d - 1))

    def i_up():
        return remote(img.at[pl.ds(1, 4)], ih.at[pl.ds(0, 4)], sh.at[IB], rh.at[IB], (s, d + 1))

    def across_dn_x(go):
        @pl.when(has_prev)
        def _():
            @pl.when(cross_up)
            def _():
                go(x_dn(high_p, YA, CA1))

            @pl.when(cross_lo)
            def _():
                go(x_dn(low_p, YA, CB1))

    def across_up_x(go):
        @pl.when(has_next)
        def _():
            @pl.when(cross_up)
            def _():
                go(x_up(high_p, YB, CA0))

            @pl.when(cross_lo)
            def _():
                go(x_up(low_p, YB, CB0))

    def halo_start():
        @pl.when(near_lo)
        def _():
            z_dn(ext, ZA).start()

        @pl.when(near_up)
        def _():
            z_up(ext, ZB).start()

        @pl.when(has_prev)
        def _():
            x_dn(core_p, XA, XA).start()

        @pl.when(has_next)
        def _():
            x_up(core_p, XB, XB).start()

        for k in range(1, NSUB):
            weight_out(k).start()

        @pl.when(has_next)
        def _():
            x_dn(core_p, XA, XA).wait_recv()

            @pl.when(near_lo)
            def _():
                z_dn(ext_bot, CA1).start()

            @pl.when(near_up)
            def _():
                z_up(ext_bot, CB1).start()

        @pl.when(has_prev)
        def _():
            x_up(core_p, XB, XB).wait_recv()

            @pl.when(near_lo)
            def _():
                z_dn(ext_top, CA0).start()

            @pl.when(near_up)
            def _():
                z_up(ext_top, CB0).start()

        b_flat = b_buf.reshape(NSUB * 4 * ROWS, Y)

        def far_end(side, base):
            for k in range(NSUB):
                far_in(k, side).wait_recv()
            for p in range(4):
                for r in range(ROWS):
                    ext[r, base + p] = b_flat[pl.ds(p * ROWS + r, NSUB, stride=4 * ROWS), :]

        @pl.when(cross_lo)
        def _():
            far_end(d - 1, 0)

        @pl.when(cross_up)
        def _():
            far_end(d + 1, RAD + ZD)

        across_dn_x(lambda copy: copy.start())
        across_up_x(lambda copy: copy.start())

        @pl.when(near_up)
        def _():
            z_dn(ext, ZA).wait_recv()

        @pl.when(near_lo)
        def _():
            z_up(ext, ZB).wait_recv()

        @pl.when(near_lo)
        def _():
            i_dn().start()

        @pl.when(near_up)
        def _():
            i_up().start()

    def slab_out(k, first):
        to = peer_to(k)
        return remote(b_buf.at[to], ih.at[pl.ds(first, 4), c], sg.at[k], rg.at[c], (to, d))

    def slab_in(k, first):
        frm = peer_from(k)
        chunk = chunk_of(frm, hi)
        return remote(b_buf.at[frm], ih.at[pl.ds(first, 4), chunk], sg.at[k], rg.at[chunk], (frm, d))

    def slab_start(first):
        for k in range(1, NSUB):
            slab_out(k, first).start()
        ih[pl.ds(first, 4), c] = b_buf[s]

    def slabs():
        @pl.when(cross_lo)
        def _():
            slab_start(0)

        @pl.when(cross_up)
        def _():
            slab_start(4)

    def corners_end():
        @pl.when(has_up)
        def _():
            @pl.when(has_prev)
            def _():
                z_dn(ext_top, CA0).wait_recv()

            @pl.when(has_next)
            def _():
                z_dn(ext_bot, CA1).wait_recv()

        @pl.when(has_lo)
        def _():
            @pl.when(has_prev)
            def _():
                z_up(ext_top, CB0).wait_recv()

            @pl.when(has_next)
            def _():
                z_up(ext_bot, CB1).wait_recv()

    refs = [idx_ref[r] for r in range(NREF)]

    def depth_pass(block, first, row, carry):
        at = row + first
        vals = [block[row, p] for p in range(EXT_P)]
        for k, total in enumerate(window_depth(vals)):
            zs[0, at, k] = total
        for k, total in enumerate(window_depth([v * v for v in vals])):
            zs[1, at, k] = total
        for r in range(NREF):
            prods = [vals[p] * block[row, p, pl.ds(refs[r], 1), :] for p in range(EXT_P)]
            for k, total in enumerate(window_depth(prods)):
                zs[2 + r, at, k] = total
        return carry

    def row_pass(f, carry):
        for k in range(ZD):
            for r, total in enumerate(window_rows([zs[f, row, k] for row in range(EXT_R)])):
                xs[f * CELLS + r * ZD + k] = total
        return carry

    def core_rows():
        lax.fori_loop(0, ROWS, functools.partial(depth_pass, ext, RAD), 0)

    def other_rows():
        lax.fori_loop(0, RAD, functools.partial(depth_pass, ext_top, 0), 0)
        lax.fori_loop(0, RAD, functools.partial(depth_pass, ext_bot, RAD + ROWS), 0)

    def boxes():
        lax.fori_loop(0, NF, row_pass, 0)
        ones = band([1.0] * WIN, jnp.bfloat16)
        ones2 = jnp.concatenate([ones, ones], axis=0)

        def lane_pass(b, carry):
            val = xs[pl.ds(b * 20, 20)].reshape(320, Y)
            high = val.astype(jnp.bfloat16)
            rest = val - high.astype(jnp.float32)
            mid = rest.astype(jnp.bfloat16)
            low = (rest - mid.astype(jnp.float32)).astype(jnp.bfloat16)
            total = jnp.dot(jnp.concatenate([high, mid], axis=1), ones2, preferred_element_type=jnp.float32)
            total = total + jnp.dot(low, ones, preferred_element_type=jnp.float32)
            bx[pl.ds(b * 20, 20)] = (total * (1.0 / WIN**3)).reshape(20, NSUB, Y)
            return carry

        lax.fori_loop(0, NF * CELLS // 20, lane_pass, 0)

    def combined():
        def stats(r, carry):
            for k in range(ZD):
                q = r * ZD + k
                mean = bx[q]
                inv[q] = 1.0 / (bx[CELLS + q] - mean * mean + 1e-5)
                dev[q] = ext[r, RAD + k] - mean
            return carry

        lax.fori_loop(0, ROWS, stats, 0)
        for k in range(1, NSUB):
            weight_in(k).wait_recv()
        w_flat = w_buf.reshape(NSUB * 8, 128)
        weights = [w_flat[pl.ds(r, NSUB, stride=8), :] for r in range(NREF)]

        def combine(row, carry):
            for k in range(ZD):
                q = row * ZD + k
                mean_i, inv_i, dev_i = bx[q], inv[q], dev[q]
                total = None
                for r in range(NREF):
                    one = pl.ds(refs[r], 1)
                    gain = (bx[(2 + r) * CELLS + q] - mean_i * bx[q, one, :]) * inv_i
                    term = (2.0 * gain * inv[q, one, :]) * (dev[q, one, :] - gain * dev_i) * weights[r]
                    total = term if total is None else total + term
                c_buf[pl.ds(q * NSUB, NSUB), :] = total
            return carry

        lax.fori_loop(0, ROWS, combine, 0)
        for sub in range(NSUB):
            for p in range(ZD):
                cs[sub, p] = c_buf[pl.ds(p * NSUB + sub, ROWS, stride=ZD * NSUB), :]

    planes = pl.ds(RG, ZD)

    y_at, x_at = s // 4, s % 4
    pairs = [(j, i) for j in range(4) for i in range(4) if (j, i) != (0, 0)]

    def back_out(j, i):
        to = 4 * ((y_at + j) % 4) + (x_at + i) % 4
        return remote(cs.at[to], cf.at[planes, c], sr.at[4 * j + i], rr.at[c], (to, d))

    def back_in(j, i):
        frm = 4 * ((y_at + 4 - j) % 4) + (x_at + 4 - i) % 4
        chunk = chunk_of(frm, hi)
        return remote(cs.at[frm], cf.at[planes, chunk], sr.at[4 * j + i], rr.at[chunk], (frm, d))

    def over_up(k):
        to = peer_to(k)
        return remote(cs.at[to, pl.ds(2, RG)], cf.at[pl.ds(0, RG), c], sc.at[k], rc.at[c], (to, d + 1))

    def over_dn(k):
        to = peer_to(k)
        return remote(cs.at[to, pl.ds(0, RG)], cf.at[pl.ds(RG + ZD, RG), c], sc.at[k], rc.at[c], (to, d - 1))

    def over_in(k, first, side):
        return remote(cs.at[k, pl.ds(0, RG)], cf.at[pl.ds(first, RG), k], sc.at[k], rc.at[k], (s, side))

    def four(j):
        return pl.ds(chunk_of(4 * ((y_at + 4 - j) % 4), hi) // 4 * 4, 4)

    def f_dn(j):
        return remote(
            cf.at[pl.ds(RG, RG), four(j)], cf.at[pl.ds(RG + ZD, RG), four(j)], sh.at[FA + j], rh.at[FA + j], (s, d - 1)
        )

    def f_up(j):
        return remote(cf.at[pl.ds(ZD, RG), four(j)], cf.at[pl.ds(0, RG), four(j)], sh.at[FB + j], rh.at[FB + j], (s, d + 1))

    def home_start():
        @pl.when(cross_up)
        def _():
            for k in range(NSUB):
                over_up(k).start()

        @pl.when(cross_lo)
        def _():
            for k in range(NSUB):
                over_dn(k).start()

        for j, i in pairs:
            back_out(j, i).start()
        cf[planes, c] = cs[s]

    def home_end():
        for j in range(4):
            for i in range(4):
                if (j, i) != (0, 0):
                    back_in(j, i).wait_recv()

            @pl.when(near_lo)
            def _():
                f_dn(j).start()

            @pl.when(near_up)
            def _():
                f_up(j).start()

    taps = gauss_taps()
    lane = lax.broadcasted_iota(jnp.int32, (X, Y), 1)
    line = lax.broadcasted_iota(jnp.int32, (X, Y), 0)

    def plane(i):
        if i < 4:
            return ih[i].reshape(X, Y)
        if i < 4 + ZD:
            return img[i - 4].reshape(X, Y)
        return ih[i - ZD].reshape(X, Y)

    def gradients():
        @pl.when(near_lo)
        def _():
            i_up().wait_recv()

        @pl.when(near_up)
        def _():
            i_dn().wait_recv()

        @pl.when(cross_lo)
        def _():
            for k in range(1, NSUB):
                slab_in(k, 0).wait_recv()

        @pl.when(cross_up)
        def _():
            for k in range(1, NSUB):
                slab_in(k, 4).wait_recv()

        for p in range(FP):
            here = plane(p + 1)
            grad[0, p] = (plane(p + 2) - plane(p)) * 0.5
            below = jnp.where(line == X - 1, 0.0, pltpu.roll(here, X - 1, 0))
            above = jnp.where(line == 0, 0.0, pltpu.roll(here, 1, 0))
            grad[1, p] = (below - above) * 0.5
            after = jnp.where(lane == Y - 1, 0.0, pltpu.roll(here, Y - 1, 1))
            before = jnp.where(lane == 0, 0.0, pltpu.roll(here, 1, 1))
            grad[2, p] = (after - before) * 0.5

    def depth_sum(comp, p, inner):
        total = None
        for k in range(2 * RG + 1):
            q = p + k
            if (RG <= q < RG + ZD) == inner:
                term = (taps[k] * cf[q].reshape(X, Y)) * grad[comp, q]
                total = term if total is None else total + term
        return total

    def inner_part():
        def body(comp, carry):
            for p in range(ZD):
                part[comp, p] = depth_sum(comp, p, True)
            return carry

        lax.fori_loop(0, 3, body, 0)

    def halo_part():
        @pl.when(near_lo)
        def _():
            for j in range(4):
                f_up(j).wait_recv()

        @pl.when(near_up)
        def _():
            for j in range(4):
                f_dn(j).wait_recv()

        @pl.when(cross_up)
        def _():
            for k in range(NSUB):
                over_in(k, RG + ZD, d + 1).wait_recv()

        @pl.when(cross_lo)
        def _():
            for k in range(NSUB):
                over_in(k, 0, d - 1).wait_recv()

        matrix = band(taps, jnp.float32)
        t_high = matrix.astype(jnp.bfloat16)
        t_low = (matrix - t_high.astype(jnp.float32)).astype(jnp.bfloat16)
        none = jnp.zeros((128, 128), jnp.bfloat16)
        right = jnp.concatenate(
            [jnp.concatenate([t_high, t_low], axis=1), jnp.concatenate([t_high, none], axis=1)], axis=0
        )
        left = jnp.concatenate(
            [jnp.concatenate([t_high, t_high], axis=1), jnp.concatenate([t_low, none], axis=1)], axis=0
        )

        def split(val):
            high = val.astype(jnp.bfloat16)
            return high, (val - high.astype(jnp.float32)).astype(jnp.bfloat16)

        def body(comp, carry):
            for p in range(ZD):
                total = part[comp, p] + depth_sum(comp, p, False)
                both = jnp.dot(jnp.concatenate(split(total), axis=1), right, preferred_element_type=jnp.float32)
                across = both[:, :Y] + both[:, Y:]
                both = jnp.dot(left, jnp.concatenate(split(across), axis=0), preferred_element_type=jnp.float32)
                out[comp, p] = 40.0 * (both[:X] + both[X:])
            return carry

        lax.fori_loop(0, 3, body, 0)

    def halo_drain():
        @pl.when(has_prev)
        def _():
            x_dn(core_p, XA, XA).wait_send()

        @pl.when(has_next)
        def _():
            x_up(core_p, XB, XB).wait_send()

        across_dn_x(lambda copy: copy.wait_send())
        across_up_x(lambda copy: copy.wait_send())

        @pl.when(near_lo)
        def _():
            i_dn().wait_send()
            z_dn(ext, ZA).wait_send()

            @pl.when(has_prev)
            def _():
                z_dn(ext_top, CA0).wait_send()

            @pl.when(has_next)
            def _():
                z_dn(ext_bot, CA1).wait_send()

        @pl.when(near_up)
        def _():
            i_up().wait_send()
            z_up(ext, ZB).wait_send()

            @pl.when(has_prev)
            def _():
                z_up(ext_top, CB0).wait_send()

            @pl.when(has_next)
            def _():
                z_up(ext_bot, CB1).wait_send()

    def slab_drain():
        def both(first):
            for k in range(1, NSUB):
                slab_out(k, first).wait_send()

        @pl.when(cross_lo)
        def _():
            both(0)

        @pl.when(cross_up)
        def _():
            both(4)

    def spread_drain():
        for k in range(1, NSUB):
            chunk_out(k).wait_send()
            weight_out(k).wait_send()

        @pl.when(cross_up)
        def _():
            for k in range(NSUB):
                far_out(k, 1, d + 1).wait_send()

        @pl.when(cross_lo)
        def _():
            for k in range(NSUB):
                far_out(k, 0, d - 1).wait_send()

    def home_drain():
        for j, i in pairs:
            back_out(j, i).wait_send()

        @pl.when(cross_up)
        def _():
            for k in range(NSUB):
                over_up(k).wait_send()

        @pl.when(cross_lo)
        def _():
            for k in range(NSUB):
                over_dn(k).wait_send()

        @pl.when(near_lo)
        def _():
            for j in range(4):
                f_dn(j).wait_send()

        @pl.when(near_up)
        def _():
            for j in range(4):
                f_up(j).wait_send()

    spread()
    halo_start()
    slabs()
    core_rows()
    corners_end()
    other_rows()
    boxes()
    combined()
    home_start()
    gradients()
    spread_drain()
    halo_drain()
    slab_drain()
    home_end()
    inner_part()
    halo_part()
    home_drain()


def on_device(images, velocity, ref_index, ref_weights):
    vmem = pl.BlockSpec(memory_space=pltpu.VMEM)
    smem = pl.BlockSpec(memory_space=pltpu.SMEM)
    f32 = jnp.float32
    dma = pltpu.SemaphoreType.DMA
    smooth = pl.pallas_call(
        coeff_kernel,
        out_shape=jax.ShapeDtypeStruct((3, ZD, X, Y), f32),
        in_specs=[smem, smem, pl.BlockSpec(memory_space=pltpu.HBM)],
        out_specs=vmem,
        scratch_shapes=[
            pltpu.VMEM((ZD, NSUB, ROWS, Y), f32),
            pltpu.VMEM((NSUB, ZD, ROWS, Y), f32),
            pltpu.VMEM((NSUB, 8, 128), f32),
            pltpu.VMEM((ROWS, EXT_P, NSUB, Y), f32),
            pltpu.VMEM((RAD, EXT_P, NSUB, Y), f32),
            pltpu.VMEM((RAD, EXT_P, NSUB, Y), f32),
            pltpu.VMEM((NF, EXT_R, ZD, NSUB, Y), f32),
            pltpu.VMEM((NF * CELLS, NSUB, Y), f32),
            pltpu.VMEM((NF * CELLS, NSUB, Y), f32),
            pltpu.VMEM((CELLS, NSUB, Y), f32),
            pltpu.VMEM((CELLS, NSUB, Y), f32),
            pltpu.VMEM((CELLS * NSUB, Y), f32),
            pltpu.VMEM((NSUB, ZD, ROWS, Y), f32),
            pltpu.VMEM((NSUB, 4, ROWS, Y), f32),
            pltpu.VMEM((FP, NSUB, ROWS, Y), f32),
            pltpu.VMEM((8, NSUB, ROWS, Y), f32),
            pltpu.VMEM((3, FP, X, Y), f32),
            pltpu.VMEM((3, ZD, X, Y), f32),
            dma((NSUB,)), dma((NSUB,)), dma((NSUB,)), dma((NSUB,)), dma((NSUB,)), dma((NSUB,)),
            dma((NSUB,)), dma((NSUB,)), dma((NSUB,)), dma((NSUB,)), dma((NSUB,)), dma((NSUB,)),
            dma((20,)), dma((20,)), dma,
        ],
        compiler_params=pltpu.CompilerParams(
            collective_id=0, has_side_effects=True, vmem_limit_bytes=VLIM * 1024 * 1024
        ),
    )(ref_index, ref_weights, images.reshape(ZD, NSUB, ROWS, Y))
    return velocity + smooth.reshape(3, 1, ZD, X, Y)


def solution(mesh):
    placed = (
        P("subj", "depth", None, None),
        P(None, "subj", "depth", None, None),
        P(),
        P("subj", None),
    )
    return jax.shard_map(
        on_device,
        mesh=mesh,
        in_specs=placed,
        out_specs=P(None, "subj", "depth", None, None),
        check_vma=False,
    )
```

```python
import functools
import math

import jax
import jax.numpy as jnp
from jax import lax
from jax.experimental import pallas as pl
from jax.experimental.pallas import tpu as pltpu
from jax.sharding import PartitionSpec as P

X = 128
Y = 128
ZD = 5
NSUB = 16
NREF = 4
WIN = 9
RG = 3
WDEN = 16
RAD = WIN // 2
ROWS = X // NSUB
EXT_R = ROWS + 2 * RAD
EXT_P = ZD + 2 * RAD
CELLS = ROWS * ZD
NF = 2 + NREF
FP = ZD + 2 * RG
VLIM = 32
MESH = pl.DeviceIdType.MESH

XA, XB, ZA, ZB, CA0, CA1, CB0, CB1, IA, IB, YA, YB, FA, FB = list(range(13)) + [16]


def gauss_taps():
    raw = [math.exp(-0.5 * offset * offset) for offset in range(-RG, RG + 1)]
    total = sum(raw)
    return [value / total for value in raw]


def chunk_of(s, hi):
    y, x = s // 4, s % 4
    ys = y + hi * (3 - 2 * y)
    return 4 * ys + x + (ys % 2) * (3 - 2 * x)


def subject_of(c, hi):
    ys, xs = c // 4, c % 4
    x = xs + (ys % 2) * (3 - 2 * xs)
    return 4 * (ys + hi * (3 - 2 * ys)) + x


def window_depth(v):
    core = ((v[4] + v[5]) + (v[6] + v[7])) + v[8]
    suf2 = v[2] + v[3]
    suf1 = v[1] + suf2
    suf0 = v[0] + suf1
    pre2 = v[9] + v[10]
    pre3 = pre2 + v[11]
    pre4 = pre3 + v[12]
    return [core + suf0, (core + suf1) + v[9], (core + suf2) + pre2, (core + v[3]) + pre3, core + pre4]


def window_rows(v):
    suf = [None] * 8
    pre = [None] * 8
    suf[7] = v[7]
    pre[0] = v[8]
    for i in range(6, -1, -1):
        suf[i] = v[i] + suf[i + 1]
    for i in range(1, 8):
        pre[i] = pre[i - 1] + v[8 + i]
    return [suf[i] + pre[i] for i in range(8)]


def band(taps, dtype):
    radius = len(taps) // 2
    diff = lax.broadcasted_iota(jnp.int32, (128, 128), 0) - lax.broadcasted_iota(jnp.int32, (128, 128), 1)
    matrix = jnp.zeros((128, 128), jnp.float32)
    for offset in range(len(taps)):
        matrix = jnp.where(diff == offset - radius, taps[offset], matrix)
    return matrix.astype(dtype)


def coeff_kernel(
    idx_ref, w_ref, img_hbm, out,
    img, a_buf, w_buf, ext, ext_top, ext_bot, zs, xs, bx, inv, dev, c_buf, cs, b_buf, cf, ih, grad, part,
    sa, ra, sw, rw, sr, rr, sb, rb, sg, rg, sc, rc, sh, rh, load_sem,
):
    s = lax.axis_index("subj")
    d = lax.axis_index("depth")
    nd = lax.axis_size("depth")
    half = nd // 2
    hi = d // half
    c = chunk_of(s, hi)
    has_lo, has_up = d > 0, d < nd - 1
    cross_lo, cross_up = d == half, d == half - 1
    near_lo, near_up = has_lo & (d != half), has_up & (d != half - 1)
    has_prev, has_next = c > 0, c < NSUB - 1
    load = pltpu.make_async_copy(img_hbm, img, load_sem)
    load.start()

    barrier = pltpu.get_barrier_semaphore()
    for k in range(1, NSUB):
        pl.semaphore_signal(barrier, inc=1, device_id=((s + k) % NSUB, d), device_id_type=MESH)

    @pl.when(near_lo)
    def _():
        pl.semaphore_signal(barrier, inc=1, device_id=(s, d - 1), device_id_type=MESH)

    @pl.when(near_up)
    def _():
        pl.semaphore_signal(barrier, inc=1, device_id=(s, d + 1), device_id_type=MESH)

    @pl.when(cross_lo)
    def _():
        for k in range(NSUB):
            pl.semaphore_signal(barrier, inc=1, device_id=((s + k) % NSUB, d - 1), device_id_type=MESH)

    @pl.when(cross_up)
    def _():
        for k in range(NSUB):
            pl.semaphore_signal(barrier, inc=1, device_id=((s + k) % NSUB, d + 1), device_id_type=MESH)

    rows = lax.broadcasted_iota(jnp.int32, (8, 128), 0)
    wt = jnp.zeros((8, 128), jnp.float32)
    for r in range(NREF):
        wt = jnp.where(rows == r, w_ref[0, r].astype(jnp.float32) * (1.0 / WDEN), wt)
    w_buf[s] = wt

    @pl.when(c == 0)
    def _():
        ext_top[...] = jnp.zeros((RAD, EXT_P, NSUB, Y), jnp.float32)

    @pl.when(c == NSUB - 1)
    def _():
        ext_bot[...] = jnp.zeros((RAD, EXT_P, NSUB, Y), jnp.float32)

    @pl.when(jnp.logical_not(has_lo))
    def _():
        ext[:, 0:RAD] = jnp.zeros((ROWS, RAD, NSUB, Y), jnp.float32)
        ext_top[:, 0:RAD] = jnp.zeros((RAD, RAD, NSUB, Y), jnp.float32)
        ext_bot[:, 0:RAD] = jnp.zeros((RAD, RAD, NSUB, Y), jnp.float32)
        ih[0:4] = jnp.zeros((4, NSUB, ROWS, Y), jnp.float32)
        cf[0:RG] = jnp.zeros((RG, NSUB, ROWS, Y), jnp.float32)

    @pl.when(jnp.logical_not(has_up))
    def _():
        ext[:, RAD + ZD:] = jnp.zeros((ROWS, RAD, NSUB, Y), jnp.float32)
        ext_top[:, RAD + ZD:] = jnp.zeros((RAD, RAD, NSUB, Y), jnp.float32)
        ext_bot[:, RAD + ZD:] = jnp.zeros((RAD, RAD, NSUB, Y), jnp.float32)
        ih[4:8] = jnp.zeros((4, NSUB, ROWS, Y), jnp.float32)
        cf[RG + ZD:] = jnp.zeros((RG, NSUB, ROWS, Y), jnp.float32)

    load.wait()
    one_if = lambda cond: cond.astype(jnp.int32)
    extra = one_if(near_lo) + one_if(near_up) + NSUB * (one_if(cross_lo) + one_if(cross_up))
    pl.semaphore_wait(barrier, NSUB - 1 + extra)

    def remote(src, dst, send, recv, device):
        return pltpu.make_async_remote_copy(
            src_ref=src, dst_ref=dst, send_sem=send, recv_sem=recv, device_id=device, device_id_type=MESH
        )

    def peer_to(k):
        return (s + k) % NSUB

    def peer_from(k):
        return (s + NSUB - k) % NSUB

    def chunk_out(k):
        to = peer_to(k)
        return remote(img.at[:, chunk_of(to, hi)], a_buf.at[s], sa.at[k], ra.at[s], (to, d))

    def chunk_in(k):
        frm = peer_from(k)
        return remote(img.at[:, 0], a_buf.at[frm], sa.at[k], ra.at[frm], (frm, d))

    def weight_out(k):
        return remote(w_buf.at[s], w_buf.at[s], sw.at[k], rw.at[s], (peer_to(k), d))

    def weight_in(k):
        frm = peer_from(k)
        return remote(w_buf.at[frm], w_buf.at[frm], sw.at[k], rw.at[frm], (frm, d))

    def far_out(k, first, side):
        to = peer_to(k)
        return remote(img.at[pl.ds(first, 4), chunk_of(to, 1 - hi)], b_buf.at[s], sb.at[k], rb.at[s], (to, side))

    def far_in(k, side):
        return remote(b_buf.at[k], b_buf.at[k], sb.at[k], rb.at[k], (s, side))

    def spread():
        for k in range(1, NSUB):
            chunk_out(k).start()

        @pl.when(cross_up)
        def _():
            for k in range(NSUB):
                far_out(k, 1, d + 1).start()

        @pl.when(cross_lo)
        def _():
            for k in range(NSUB):
                far_out(k, 0, d - 1).start()

        a_buf[s] = img[:, c]
        for k in range(1, NSUB):
            chunk_in(k).wait_recv()
        a_flat = a_buf.reshape(NSUB * ZD * ROWS, Y)
        for p in range(ZD):
            for r in range(ROWS):
                ext[r, RAD + p] = a_flat[pl.ds(p * ROWS + r, NSUB, stride=ZD * ROWS), :]

    prev, nxt = subject_of(jnp.maximum(c - 1, 0), hi), subject_of(jnp.minimum(c + 1, NSUB - 1), hi)
    core_p = pl.ds(RAD, ZD)
    low_p, high_p = pl.ds(0, RAD), pl.ds(RAD + ZD, RAD)

    def x_dn(planes, send, recv):
        return remote(ext.at[pl.ds(0, RAD), planes], ext_bot.at[:, planes], sh.at[send], rh.at[recv], (prev, d))

    def x_up(planes, send, recv):
        return remote(ext.at[pl.ds(RAD, RAD), planes], ext_top.at[:, planes], sh.at[send], rh.at[recv], (nxt, d))

    def z_dn(block, sem):
        return remote(block.at[:, pl.ds(RAD, RAD)], block.at[:, high_p], sh.at[sem], rh.at[sem], (s, d - 1))

    def z_up(block, sem):
        return remote(block.at[:, pl.ds(ZD, RAD)], block.at[:, low_p], sh.at[sem], rh.at[sem], (s, d + 1))

    def i_dn():
        return remote(img.at[pl.ds(0, 4)], ih.at[pl.ds(4, 4)], sh.at[IA], rh.at[IA], (s, d - 1))

    def i_up():
        return remote(img.at[pl.ds(1, 4)], ih.at[pl.ds(0, 4)], sh.at[IB], rh.at[IB], (s, d + 1))

    def across_dn_x(go):
        @pl.when(has_prev)
        def _():
            @pl.when(cross_up)
            def _():
                go(x_dn(high_p, YA, CA1))

            @pl.when(cross_lo)
            def _():
                go(x_dn(low_p, YA, CB1))

    def across_up_x(go):
        @pl.when(has_next)
        def _():
            @pl.when(cross_up)
            def _():
                go(x_up(high_p, YB, CA0))

            @pl.when(cross_lo)
            def _():
                go(x_up(low_p, YB, CB0))

    def halo_start():
        @pl.when(near_lo)
        def _():
            z_dn(ext, ZA).start()

        @pl.when(near_up)
        def _():
            z_up(ext, ZB).start()

        @pl.when(has_prev)
        def _():
            x_dn(core_p, XA, XA).start()

        @pl.when(has_next)
        def _():
            x_up(core_p, XB, XB).start()

        for k in range(1, NSUB):
            weight_out(k).start()

        @pl.when(has_next)
        def _():
            x_dn(core_p, XA, XA).wait_recv()

            @pl.when(near_lo)
            def _():
                z_dn(ext_bot, CA1).start()

            @pl.when(near_up)
            def _():
                z_up(ext_bot, CB1).start()

        @pl.when(has_prev)
        def _():
            x_up(core_p, XB, XB).wait_recv()

            @pl.when(near_lo)
            def _():
                z_dn(ext_top, CA0).start()

            @pl.when(near_up)
            def _():
                z_up(ext_top, CB0).start()

        b_flat = b_buf.reshape(NSUB * 4 * ROWS, Y)

        def far_end(side, base):
            for k in range(NSUB):
                far_in(k, side).wait_recv()
            for p in range(4):
                for r in range(ROWS):
                    ext[r, base + p] = b_flat[pl.ds(p * ROWS + r, NSUB, stride=4 * ROWS), :]

        @pl.when(cross_lo)
        def _():
            far_end(d - 1, 0)

        @pl.when(cross_up)
        def _():
            far_end(d + 1, RAD + ZD)

        across_dn_x(lambda copy: copy.start())
        across_up_x(lambda copy: copy.start())

        @pl.when(near_up)
        def _():
            z_dn(ext, ZA).wait_recv()

        @pl.when(near_lo)
        def _():
            z_up(ext, ZB).wait_recv()

        @pl.when(near_lo)
        def _():
            i_dn().start()

        @pl.when(near_up)
        def _():
            i_up().start()

    def slab_out(k, first):
        to = peer_to(k)
        return remote(b_buf.at[to], ih.at[pl.ds(first, 4), c], sg.at[k], rg.at[c], (to, d))

    def slab_in(k, first):
        frm = peer_from(k)
        chunk = chunk_of(frm, hi)
        return remote(b_buf.at[frm], ih.at[pl.ds(first, 4), chunk], sg.at[k], rg.at[chunk], (frm, d))

    def slab_start(first):
        for k in range(1, NSUB):
            slab_out(k, first).start()
        ih[pl.ds(first, 4), c] = b_buf[s]

    def slabs():
        @pl.when(cross_lo)
        def _():
            slab_start(0)

        @pl.when(cross_up)
        def _():
            slab_start(4)

    def corners_end():
        @pl.when(has_up)
        def _():
            @pl.when(has_prev)
            def _():
                z_dn(ext_top, CA0).wait_recv()

            @pl.when(has_next)
            def _():
                z_dn(ext_bot, CA1).wait_recv()

        @pl.when(has_lo)
        def _():
            @pl.when(has_prev)
            def _():
                z_up(ext_top, CB0).wait_recv()

            @pl.when(has_next)
            def _():
                z_up(ext_bot, CB1).wait_recv()

    refs = [idx_ref[r] for r in range(NREF)]

    def depth_pass(block, first, row, carry):
        at = row + first
        vals = [block[row, p] for p in range(EXT_P)]
        for k, total in enumerate(window_depth(vals)):
            zs[0, at, k] = total
        for k, total in enumerate(window_depth([v * v for v in vals])):
            zs[1, at, k] = total
        for r in range(NREF):
            prods = [vals[p] * block[row, p, pl.ds(refs[r], 1), :] for p in range(EXT_P)]
            for k, total in enumerate(window_depth(prods)):
                zs[2 + r, at, k] = total
        return carry

    odd = d % 2
    parts = ((2 * odd, 3), (3 - 3 * odd, 2))

    def row_pass(base, n, f, carry):
        for k in range(n):
            at = base + k
            for r, total in enumerate(window_rows([zs[f, row, at] for row in range(EXT_R)])):
                xs[(f * ZD + at) * ROWS + r] = total
        return carry

    def core_rows():
        lax.fori_loop(0, ROWS, functools.partial(depth_pass, ext, RAD), 0)

    def other_rows():
        lax.fori_loop(0, RAD, functools.partial(depth_pass, ext_top, 0), 0)
        lax.fori_loop(0, RAD, functools.partial(depth_pass, ext_bot, RAD + ROWS), 0)

    def boxes(base, n):
        lax.fori_loop(0, NF, functools.partial(row_pass, base, n), 0)
        ones = band([1.0] * WIN, jnp.bfloat16)
        ones2 = jnp.concatenate([ones, ones], axis=0)
        size = n * ROWS

        def lane_pass(f, carry):
            block = pl.ds((f * ZD + base) * ROWS, size)
            val = xs[block].reshape(size * NSUB, Y)
            high = val.astype(jnp.bfloat16)
            rest = val - high.astype(jnp.float32)
            mid = rest.astype(jnp.bfloat16)
            low = (rest - mid.astype(jnp.float32)).astype(jnp.bfloat16)
            total = jnp.dot(jnp.concatenate([high, mid], axis=1), ones2, preferred_element_type=jnp.float32)
            total = total + jnp.dot(low, ones, preferred_element_type=jnp.float32)
            bx[block] = (total * (1.0 / WIN**3)).reshape(size, NSUB, Y)
            return carry

        lax.fori_loop(0, NF, lane_pass, 0)

    def combined(base, n):
        def stats(r, carry):
            for k in range(n):
                q = (base + k) * ROWS + r
                mean = bx[q]
                inv[q] = 1.0 / (bx[CELLS + q] - mean * mean + 1e-5)
                dev[q] = ext[r, RAD + base + k] - mean
            return carry

        lax.fori_loop(0, ROWS, stats, 0)
        w_flat = w_buf.reshape(NSUB * 8, 128)
        weights = [w_flat[pl.ds(r, NSUB, stride=8), :] for r in range(NREF)]

        def combine(row, carry):
            for k in range(n):
                q = (base + k) * ROWS + row
                mean_i, inv_i, dev_i = bx[q], inv[q], dev[q]
                total = None
                for r in range(NREF):
                    one = pl.ds(refs[r], 1)
                    gain = (bx[(2 + r) * CELLS + q] - mean_i * bx[q, one, :]) * inv_i
                    term = (2.0 * gain * inv[q, one, :]) * (dev[q, one, :] - gain * dev_i) * weights[r]
                    total = term if total is None else total + term
                c_buf[pl.ds((k * ROWS + row) * NSUB, NSUB), :] = total
            return carry

        lax.fori_loop(0, ROWS, combine, 0)
        for sub in range(NSUB):
            for k in range(n):
                cs[sub, base + k] = c_buf[pl.ds(k * ROWS * NSUB + sub, ROWS, stride=NSUB), :]

    def weights_end():
        for k in range(1, NSUB):
            weight_in(k).wait_recv()


    y_at, x_at = s // 4, s % 4
    pairs = [(j, i) for j in range(4) for i in range(4) if (j, i) != (0, 0)]

    def back_out(j, i, part):
        to = 4 * ((y_at + j) % 4) + (x_at + i) % 4
        base, n = parts[part]
        sem = part * NSUB + 4 * j + i
        return remote(
            cs.at[to, pl.ds(base, n)], cf.at[pl.ds(RG + base, n), c], sr.at[sem], rr.at[part * NSUB + c], (to, d)
        )

    def back_in(j, i, part):
        frm = 4 * ((y_at + 4 - j) % 4) + (x_at + 4 - i) % 4
        chunk = chunk_of(frm, hi)
        base, n = parts[part]
        sem = part * NSUB + 4 * j + i
        return remote(
            cs.at[frm, pl.ds(base, n)], cf.at[pl.ds(RG + base, n), chunk], sr.at[sem], rr.at[part * NSUB + chunk], (frm, d)
        )

    def over_up(k):
        to = peer_to(k)
        return remote(cs.at[to, pl.ds(2, RG)], cf.at[pl.ds(0, RG), c], sc.at[k], rc.at[c], (to, d + 1))

    def over_dn(k):
        to = peer_to(k)
        return remote(cs.at[to, pl.ds(0, RG)], cf.at[pl.ds(RG + ZD, RG), c], sc.at[k], rc.at[c], (to, d - 1))

    def over_in(k, first, side):
        return remote(cs.at[k, pl.ds(0, RG)], cf.at[pl.ds(first, RG), k], sc.at[k], rc.at[k], (s, side))

    def four(j):
        return pl.ds(chunk_of(4 * ((y_at + 4 - j) % 4), hi) // 4 * 4, 4)

    def f_dn(j):
        return remote(
            cf.at[pl.ds(RG, RG), four(j)], cf.at[pl.ds(RG + ZD, RG), four(j)], sh.at[FA + j], rh.at[FA + j], (s, d - 1)
        )

    def f_up(j):
        return remote(cf.at[pl.ds(ZD, RG), four(j)], cf.at[pl.ds(0, RG), four(j)], sh.at[FB + j], rh.at[FB + j], (s, d + 1))

    def home_start(part):
        if part == 0:
            @pl.when(cross_up)
            def _():
                for k in range(NSUB):
                    over_up(k).start()

            @pl.when(cross_lo)
            def _():
                for k in range(NSUB):
                    over_dn(k).start()

        for j, i in pairs:
            back_out(j, i, part).start()
        base, n = parts[part]
        cf[pl.ds(RG + base, n), c] = cs[s, pl.ds(base, n)]

    def home_end(part):
        for j in range(4):
            for i in range(4):
                if (j, i) != (0, 0):
                    back_in(j, i, part).wait_recv()

            @pl.when(near_lo & (odd == part))
            def _():
                f_dn(j).start()

            @pl.when(near_up & (odd == 1 - part))
            def _():
                f_up(j).start()

    taps = gauss_taps()
    lane = lax.broadcasted_iota(jnp.int32, (X, Y), 1)
    line = lax.broadcasted_iota(jnp.int32, (X, Y), 0)

    def plane(i):
        if i < 4:
            return ih[i].reshape(X, Y)
        if i < 4 + ZD:
            return img[i - 4].reshape(X, Y)
        return ih[i - ZD].reshape(X, Y)

    def gradients():
        @pl.when(near_lo)
        def _():
            i_up().wait_recv()

        @pl.when(near_up)
        def _():
            i_dn().wait_recv()

        @pl.when(cross_lo)
        def _():
            for k in range(1, NSUB):
                slab_in(k, 0).wait_recv()

        @pl.when(cross_up)
        def _():
            for k in range(1, NSUB):
                slab_in(k, 4).wait_recv()

        for p in range(FP):
            here = plane(p + 1)
            grad[0, p] = (plane(p + 2) - plane(p)) * 0.5
            below = jnp.where(line == X - 1, 0.0, pltpu.roll(here, X - 1, 0))
            above = jnp.where(line == 0, 0.0, pltpu.roll(here, 1, 0))
            grad[1, p] = (below - above) * 0.5
            after = jnp.where(lane == Y - 1, 0.0, pltpu.roll(here, Y - 1, 1))
            before = jnp.where(lane == 0, 0.0, pltpu.roll(here, 1, 1))
            grad[2, p] = (after - before) * 0.5

    def depth_sum(comp, p, inner):
        total = None
        for k in range(2 * RG + 1):
            q = p + k
            if (RG <= q < RG + ZD) == inner:
                term = (taps[k] * cf[q].reshape(X, Y)) * grad[comp, q]
                total = term if total is None else total + term
        return total

    def inner_part():
        def body(comp, carry):
            for p in range(ZD):
                part[comp, p] = depth_sum(comp, p, True)
            return carry

        lax.fori_loop(0, 3, body, 0)

    def halo_part():
        @pl.when(near_lo)
        def _():
            for j in range(4):
                f_up(j).wait_recv()

        @pl.when(near_up)
        def _():
            for j in range(4):
                f_dn(j).wait_recv()

        @pl.when(cross_up)
        def _():
            for k in range(NSUB):
                over_in(k, RG + ZD, d + 1).wait_recv()

        @pl.when(cross_lo)
        def _():
            for k in range(NSUB):
                over_in(k, 0, d - 1).wait_recv()

        matrix = band(taps, jnp.float32)
        t_high = matrix.astype(jnp.bfloat16)
        t_low = (matrix - t_high.astype(jnp.float32)).astype(jnp.bfloat16)
        none = jnp.zeros((128, 128), jnp.bfloat16)
        right = jnp.concatenate(
            [jnp.concatenate([t_high, t_low], axis=1), jnp.concatenate([t_high, none], axis=1)], axis=0
        )
        left = jnp.concatenate(
            [jnp.concatenate([t_high, t_high], axis=1), jnp.concatenate([t_low, none], axis=1)], axis=0
        )

        def split(val):
            high = val.astype(jnp.bfloat16)
            return high, (val - high.astype(jnp.float32)).astype(jnp.bfloat16)

        def body(comp, carry):
            for p in range(ZD):
                total = part[comp, p] + depth_sum(comp, p, False)
                both = jnp.dot(jnp.concatenate(split(total), axis=1), right, preferred_element_type=jnp.float32)
                across = both[:, :Y] + both[:, Y:]
                both = jnp.dot(left, jnp.concatenate(split(across), axis=0), preferred_element_type=jnp.float32)
                out[comp, p] = 40.0 * (both[:X] + both[X:])
            return carry

        lax.fori_loop(0, 3, body, 0)

    def halo_drain():
        @pl.when(has_prev)
        def _():
            x_dn(core_p, XA, XA).wait_send()

        @pl.when(has_next)
        def _():
            x_up(core_p, XB, XB).wait_send()

        across_dn_x(lambda copy: copy.wait_send())
        across_up_x(lambda copy: copy.wait_send())

        @pl.when(near_lo)
        def _():
            i_dn().wait_send()
            z_dn(ext, ZA).wait_send()

            @pl.when(has_prev)
            def _():
                z_dn(ext_top, CA0).wait_send()

            @pl.when(has_next)
            def _():
                z_dn(ext_bot, CA1).wait_send()

        @pl.when(near_up)
        def _():
            i_up().wait_send()
            z_up(ext, ZB).wait_send()

            @pl.when(has_prev)
            def _():
                z_up(ext_top, CB0).wait_send()

            @pl.when(has_next)
            def _():
                z_up(ext_bot, CB1).wait_send()

    def slab_drain():
        def both(first):
            for k in range(1, NSUB):
                slab_out(k, first).wait_send()

        @pl.when(cross_lo)
        def _():
            both(0)

        @pl.when(cross_up)
        def _():
            both(4)

    def spread_drain():
        for k in range(1, NSUB):
            chunk_out(k).wait_send()
            weight_out(k).wait_send()

        @pl.when(cross_up)
        def _():
            for k in range(NSUB):
                far_out(k, 1, d + 1).wait_send()

        @pl.when(cross_lo)
        def _():
            for k in range(NSUB):
                far_out(k, 0, d - 1).wait_send()

    def home_drain():
        for j, i in pairs:
            back_out(j, i, 0).wait_send()
            back_out(j, i, 1).wait_send()

        @pl.when(cross_up)
        def _():
            for k in range(NSUB):
                over_up(k).wait_send()

        @pl.when(cross_lo)
        def _():
            for k in range(NSUB):
                over_dn(k).wait_send()

        @pl.when(near_lo)
        def _():
            for j in range(4):
                f_dn(j).wait_send()

        @pl.when(near_up)
        def _():
            for j in range(4):
                f_up(j).wait_send()

    spread()
    halo_start()
    slabs()
    core_rows()
    corners_end()
    other_rows()
    weights_end()
    for turn in range(2):
        boxes(*parts[turn])
        combined(*parts[turn])
        home_start(turn)
    gradients()
    spread_drain()
    halo_drain()
    slab_drain()
    home_end(0)
    home_end(1)
    inner_part()
    halo_part()
    home_drain()


def on_device(images, velocity, ref_index, ref_weights):
    vmem = pl.BlockSpec(memory_space=pltpu.VMEM)
    smem = pl.BlockSpec(memory_space=pltpu.SMEM)
    f32 = jnp.float32
    dma = pltpu.SemaphoreType.DMA
    smooth = pl.pallas_call(
        coeff_kernel,
        out_shape=jax.ShapeDtypeStruct((3, ZD, X, Y), f32),
        in_specs=[smem, smem, pl.BlockSpec(memory_space=pltpu.HBM)],
        out_specs=vmem,
        scratch_shapes=[
            pltpu.VMEM((ZD, NSUB, ROWS, Y), f32),
            pltpu.VMEM((NSUB, ZD, ROWS, Y), f32),
            pltpu.VMEM((NSUB, 8, 128), f32),
            pltpu.VMEM((ROWS, EXT_P, NSUB, Y), f32),
            pltpu.VMEM((RAD, EXT_P, NSUB, Y), f32),
            pltpu.VMEM((RAD, EXT_P, NSUB, Y), f32),
            pltpu.VMEM((NF, EXT_R, ZD, NSUB, Y), f32),
            pltpu.VMEM((NF * CELLS, NSUB, Y), f32),
            pltpu.VMEM((NF * CELLS, NSUB, Y), f32),
            pltpu.VMEM((CELLS, NSUB, Y), f32),
            pltpu.VMEM((CELLS, NSUB, Y), f32),
            pltpu.VMEM((CELLS * NSUB, Y), f32),
            pltpu.VMEM((NSUB, ZD, ROWS, Y), f32),
            pltpu.VMEM((NSUB, 4, ROWS, Y), f32),
            pltpu.VMEM((FP, NSUB, ROWS, Y), f32),
            pltpu.VMEM((8, NSUB, ROWS, Y), f32),
            pltpu.VMEM((3, FP, X, Y), f32),
            pltpu.VMEM((3, ZD, X, Y), f32),
            dma((NSUB,)), dma((NSUB,)), dma((NSUB,)), dma((NSUB,)), dma((2 * NSUB,)), dma((2 * NSUB,)),
            dma((NSUB,)), dma((NSUB,)), dma((NSUB,)), dma((NSUB,)), dma((NSUB,)), dma((NSUB,)),
            dma((20,)), dma((20,)), dma,
        ],
        compiler_params=pltpu.CompilerParams(
            collective_id=0, has_side_effects=True, vmem_limit_bytes=VLIM * 1024 * 1024
        ),
    )(pltpu.with_memory_space_constraint(ref_index, pltpu.HBM), pltpu.with_memory_space_constraint(ref_weights, pltpu.HBM), pltpu.with_memory_space_constraint(images.reshape(ZD, NSUB, ROWS, Y), pltpu.HBM))
    return velocity + smooth.reshape(3, 1, ZD, X, Y)


def solution(mesh):
    placed = (
        P("subj", "depth", None, None),
        P(None, "subj", "depth", None, None),
        P(),
        P("subj", None),
    )
    return jax.shard_map(
        on_device,
        mesh=mesh,
        in_specs=placed,
        out_specs=P(None, "subj", "depth", None, None),
        check_vma=False,
    )
```

```python
import functools
import math

import jax
import jax.numpy as jnp
from jax import lax
from jax.experimental import pallas as pl
from jax.experimental.pallas import tpu as pltpu
from jax.sharding import PartitionSpec as P

X = 128
Y = 128
ZD = 5
NSUB = 16
NREF = 4
WIN = 9
RG = 3
WDEN = 16
RAD = WIN // 2
ROWS = X // NSUB
EXT_R = ROWS + 2 * RAD
EXT_P = ZD + 2 * RAD
CELLS = ROWS * ZD
NF = 2 + NREF
FP = ZD + 2 * RG
VLIM = 32
ORDER = (4, 12, 8, 5, 13, 9, 6, 14, 10, 7, 15, 11, 1, 3, 2)
MESH = pl.DeviceIdType.MESH

XA, XB, ZA, ZB, CA0, CA1, CB0, CB1, IA, IB, YA, YB, FA, FB = list(range(13)) + [16]


def gauss_taps():
    raw = [math.exp(-0.5 * offset * offset) for offset in range(-RG, RG + 1)]
    total = sum(raw)
    return [value / total for value in raw]


def chunk_of(s, hi):
    y, x = s // 4, s % 4
    ys = y + hi * (3 - 2 * y)
    return 4 * ys + x + (ys % 2) * (3 - 2 * x)


def subject_of(c, hi):
    ys, xs = c // 4, c % 4
    x = xs + (ys % 2) * (3 - 2 * xs)
    return 4 * (ys + hi * (3 - 2 * ys)) + x


def window_depth(v):
    core = ((v[4] + v[5]) + (v[6] + v[7])) + v[8]
    suf2 = v[2] + v[3]
    suf1 = v[1] + suf2
    suf0 = v[0] + suf1
    pre2 = v[9] + v[10]
    pre3 = pre2 + v[11]
    pre4 = pre3 + v[12]
    return [core + suf0, (core + suf1) + v[9], (core + suf2) + pre2, (core + v[3]) + pre3, core + pre4]


def window_rows(v):
    suf = [None] * 8
    pre = [None] * 8
    suf[7] = v[7]
    pre[0] = v[8]
    for i in range(6, -1, -1):
        suf[i] = v[i] + suf[i + 1]
    for i in range(1, 8):
        pre[i] = pre[i - 1] + v[8 + i]
    return [suf[i] + pre[i] for i in range(8)]


def band(taps, dtype):
    radius = len(taps) // 2
    diff = lax.broadcasted_iota(jnp.int32, (128, 128), 0) - lax.broadcasted_iota(jnp.int32, (128, 128), 1)
    matrix = jnp.zeros((128, 128), jnp.float32)
    for offset in range(len(taps)):
        matrix = jnp.where(diff == offset - radius, taps[offset], matrix)
    return matrix.astype(dtype)


def coeff_kernel(
    idx_ref, w_ref, img_hbm, out,
    img, a_buf, w_buf, ext, ext_top, ext_bot, zs, xs, bx, inv, dev, c_buf, cs, b_buf, cf, ih, grad, part,
    sa, ra, sw, rw, sr, rr, sb, rb, sg, rg, sc, rc, sh, rh, load_sem,
):
    s = lax.axis_index("subj")
    d = lax.axis_index("depth")
    nd = lax.axis_size("depth")
    half = nd // 2
    hi = d // half
    c = chunk_of(s, hi)
    has_lo, has_up = d > 0, d < nd - 1
    cross_lo, cross_up = d == half, d == half - 1
    near_lo, near_up = has_lo & (d != half), has_up & (d != half - 1)
    has_prev, has_next = c > 0, c < NSUB - 1
    load = pltpu.make_async_copy(img_hbm, img, load_sem)
    load.start()

    barrier = pltpu.get_barrier_semaphore()
    for k in range(1, NSUB):
        pl.semaphore_signal(barrier, inc=1, device_id=((s + k) % NSUB, d), device_id_type=MESH)

    @pl.when(near_lo)
    def _():
        pl.semaphore_signal(barrier, inc=1, device_id=(s, d - 1), device_id_type=MESH)

    @pl.when(near_up)
    def _():
        pl.semaphore_signal(barrier, inc=1, device_id=(s, d + 1), device_id_type=MESH)

    @pl.when(cross_lo)
    def _():
        for k in range(NSUB):
            pl.semaphore_signal(barrier, inc=1, device_id=((s + k) % NSUB, d - 1), device_id_type=MESH)

    @pl.when(cross_up)
    def _():
        for k in range(NSUB):
            pl.semaphore_signal(barrier, inc=1, device_id=((s + k) % NSUB, d + 1), device_id_type=MESH)

    rows = lax.broadcasted_iota(jnp.int32, (8, 128), 0)
    wt = jnp.zeros((8, 128), jnp.float32)
    for r in range(NREF):
        wt = jnp.where(rows == r, w_ref[0, r].astype(jnp.float32) * (1.0 / WDEN), wt)
    w_buf[s] = wt

    @pl.when(c == 0)
    def _():
        ext_top[...] = jnp.zeros((RAD, EXT_P, NSUB, Y), jnp.float32)

    @pl.when(c == NSUB - 1)
    def _():
        ext_bot[...] = jnp.zeros((RAD, EXT_P, NSUB, Y), jnp.float32)

    @pl.when(jnp.logical_not(has_lo))
    def _():
        ext[:, 0:RAD] = jnp.zeros((ROWS, RAD, NSUB, Y), jnp.float32)
        ext_top[:, 0:RAD] = jnp.zeros((RAD, RAD, NSUB, Y), jnp.float32)
        ext_bot[:, 0:RAD] = jnp.zeros((RAD, RAD, NSUB, Y), jnp.float32)
        ih[0:4] = jnp.zeros((4, NSUB, ROWS, Y), jnp.float32)
        cf[0:RG] = jnp.zeros((RG, NSUB, ROWS, Y), jnp.float32)

    @pl.when(jnp.logical_not(has_up))
    def _():
        ext[:, RAD + ZD:] = jnp.zeros((ROWS, RAD, NSUB, Y), jnp.float32)
        ext_top[:, RAD + ZD:] = jnp.zeros((RAD, RAD, NSUB, Y), jnp.float32)
        ext_bot[:, RAD + ZD:] = jnp.zeros((RAD, RAD, NSUB, Y), jnp.float32)
        ih[4:8] = jnp.zeros((4, NSUB, ROWS, Y), jnp.float32)
        cf[RG + ZD:] = jnp.zeros((RG, NSUB, ROWS, Y), jnp.float32)

    load.wait()
    one_if = lambda cond: cond.astype(jnp.int32)
    extra = one_if(near_lo) + one_if(near_up) + NSUB * (one_if(cross_lo) + one_if(cross_up))
    pl.semaphore_wait(barrier, NSUB - 1 + extra)

    def remote(src, dst, send, recv, device):
        return pltpu.make_async_remote_copy(
            src_ref=src, dst_ref=dst, send_sem=send, recv_sem=recv, device_id=device, device_id_type=MESH
        )

    def peer_to(k):
        return (s + k) % NSUB

    def peer_from(k):
        return (s + NSUB - k) % NSUB

    def chunk_out(k):
        to = peer_to(k)
        return remote(img.at[:, chunk_of(to, hi)], a_buf.at[s], sa.at[k], ra.at[s], (to, d))

    def chunk_in(k):
        frm = peer_from(k)
        return remote(img.at[:, 0], a_buf.at[frm], sa.at[k], ra.at[frm], (frm, d))

    def weight_out(k):
        return remote(w_buf.at[s], w_buf.at[s], sw.at[k], rw.at[s], (peer_to(k), d))

    def weight_in(k):
        frm = peer_from(k)
        return remote(w_buf.at[frm], w_buf.at[frm], sw.at[k], rw.at[frm], (frm, d))

    def far_out(k, first, side):
        to = peer_to(k)
        return remote(img.at[pl.ds(first, 4), chunk_of(to, 1 - hi)], b_buf.at[s], sb.at[k], rb.at[s], (to, side))

    def far_in(k, side):
        return remote(b_buf.at[k], b_buf.at[k], sb.at[k], rb.at[k], (s, side))

    def spread():
        for k in ORDER:
            chunk_out(k).start()

        @pl.when(cross_up)
        def _():
            for k in range(NSUB):
                far_out(k, 1, d + 1).start()

        @pl.when(cross_lo)
        def _():
            for k in range(NSUB):
                far_out(k, 0, d - 1).start()

        a_buf[s] = img[:, c]
        for k in range(1, NSUB):
            chunk_in(k).wait_recv()
        a_flat = a_buf.reshape(NSUB * ZD * ROWS, Y)
        for p in range(ZD):
            for r in range(ROWS):
                ext[r, RAD + p] = a_flat[pl.ds(p * ROWS + r, NSUB, stride=ZD * ROWS), :]

    prev, nxt = subject_of(jnp.maximum(c - 1, 0), hi), subject_of(jnp.minimum(c + 1, NSUB - 1), hi)
    core_p = pl.ds(RAD, ZD)
    low_p, high_p = pl.ds(0, RAD), pl.ds(RAD + ZD, RAD)

    def x_dn(planes, send, recv):
        return remote(ext.at[pl.ds(0, RAD), planes], ext_bot.at[:, planes], sh.at[send], rh.at[recv], (prev, d))

    def x_up(planes, send, recv):
        return remote(ext.at[pl.ds(RAD, RAD), planes], ext_top.at[:, planes], sh.at[send], rh.at[recv], (nxt, d))

    def z_dn(block, sem):
        return remote(block.at[:, pl.ds(RAD, RAD)], block.at[:, high_p], sh.at[sem], rh.at[sem], (s, d - 1))

    def z_up(block, sem):
        return remote(block.at[:, pl.ds(ZD, RAD)], block.at[:, low_p], sh.at[sem], rh.at[sem], (s, d + 1))

    def i_dn():
        return remote(img.at[pl.ds(0, 4)], ih.at[pl.ds(4, 4)], sh.at[IA], rh.at[IA], (s, d - 1))

    def i_up():
        return remote(img.at[pl.ds(1, 4)], ih.at[pl.ds(0, 4)], sh.at[IB], rh.at[IB], (s, d + 1))

    def across_dn_x(go):
        @pl.when(has_prev)
        def _():
            @pl.when(cross_up)
            def _():
                go(x_dn(high_p, YA, CA1))

            @pl.when(cross_lo)
            def _():
                go(x_dn(low_p, YA, CB1))

    def across_up_x(go):
        @pl.when(has_next)
        def _():
            @pl.when(cross_up)
            def _():
                go(x_up(high_p, YB, CA0))

            @pl.when(cross_lo)
            def _():
                go(x_up(low_p, YB, CB0))

    def halo_start():
        @pl.when(near_lo)
        def _():
            z_dn(ext, ZA).start()

        @pl.when(near_up)
        def _():
            z_up(ext, ZB).start()

        @pl.when(has_prev)
        def _():
            x_dn(core_p, XA, XA).start()

        @pl.when(has_next)
        def _():
            x_up(core_p, XB, XB).start()

        for k in range(1, NSUB):
            weight_out(k).start()

        @pl.when(has_next)
        def _():
            x_dn(core_p, XA, XA).wait_recv()

            @pl.when(near_lo)
            def _():
                z_dn(ext_bot, CA1).start()

            @pl.when(near_up)
            def _():
                z_up(ext_bot, CB1).start()

        @pl.when(has_prev)
        def _():
            x_up(core_p, XB, XB).wait_recv()

            @pl.when(near_lo)
            def _():
                z_dn(ext_top, CA0).start()

            @pl.when(near_up)
            def _():
                z_up(ext_top, CB0).start()

        b_flat = b_buf.reshape(NSUB * 4 * ROWS, Y)

        def far_end(side, base):
            for k in range(NSUB):
                far_in(k, side).wait_recv()
            for p in range(4):
                for r in range(ROWS):
                    ext[r, base + p] = b_flat[pl.ds(p * ROWS + r, NSUB, stride=4 * ROWS), :]

        @pl.when(cross_lo)
        def _():
            far_end(d - 1, 0)

        @pl.when(cross_up)
        def _():
            far_end(d + 1, RAD + ZD)

        across_dn_x(lambda copy: copy.start())
        across_up_x(lambda copy: copy.start())

        @pl.when(near_up)
        def _():
            z_dn(ext, ZA).wait_recv()

        @pl.when(near_lo)
        def _():
            z_up(ext, ZB).wait_recv()

        @pl.when(near_lo)
        def _():
            i_dn().start()

        @pl.when(near_up)
        def _():
            i_up().start()

    def slab_out(k, first):
        to = peer_to(k)
        return remote(b_buf.at[to], ih.at[pl.ds(first, 4), c], sg.at[k], rg.at[c], (to, d))

    def slab_in(k, first):
        frm = peer_from(k)
        chunk = chunk_of(frm, hi)
        return remote(b_buf.at[frm], ih.at[pl.ds(first, 4), chunk], sg.at[k], rg.at[chunk], (frm, d))

    def slab_start(first):
        for k in range(1, NSUB):
            slab_out(k, first).start()
        ih[pl.ds(first, 4), c] = b_buf[s]

    def slabs():
        @pl.when(cross_lo)
        def _():
            slab_start(0)

        @pl.when(cross_up)
        def _():
            slab_start(4)

    def corners_end():
        @pl.when(has_up)
        def _():
            @pl.when(has_prev)
            def _():
                z_dn(ext_top, CA0).wait_recv()

            @pl.when(has_next)
            def _():
                z_dn(ext_bot, CA1).wait_recv()

        @pl.when(has_lo)
        def _():
            @pl.when(has_prev)
            def _():
                z_up(ext_top, CB0).wait_recv()

            @pl.when(has_next)
            def _():
                z_up(ext_bot, CB1).wait_recv()

    refs = [idx_ref[r] for r in range(NREF)]

    def depth_pass(block, first, row, carry):
        at = row + first
        vals = [block[row, p] for p in range(EXT_P)]
        for k, total in enumerate(window_depth(vals)):
            zs[0, at, k] = total
        for k, total in enumerate(window_depth([v * v for v in vals])):
            zs[1, at, k] = total
        for r in range(NREF):
            prods = [vals[p] * block[row, p, pl.ds(refs[r], 1), :] for p in range(EXT_P)]
            for k, total in enumerate(window_depth(prods)):
                zs[2 + r, at, k] = total
        return carry

    odd = d % 2
    parts = ((2 * odd, 3), (3 - 3 * odd, 2))

    def row_pass(base, n, f, carry):
        for k in range(n):
            at = base + k
            for r, total in enumerate(window_rows([zs[f, row, at] for row in range(EXT_R)])):
                xs[(f * ZD + at) * ROWS + r] = total
        return carry

    def core_rows():
        lax.fori_loop(0, ROWS, functools.partial(depth_pass, ext, RAD), 0)

    def other_rows():
        lax.fori_loop(0, RAD, functools.partial(depth_pass, ext_top, 0), 0)
        lax.fori_loop(0, RAD, functools.partial(depth_pass, ext_bot, RAD + ROWS), 0)

    def boxes(base, n):
        lax.fori_loop(0, NF, functools.partial(row_pass, base, n), 0)
        ones = band([1.0] * WIN, jnp.bfloat16)
        ones2 = jnp.concatenate([ones, ones], axis=0)
        size = n * ROWS

        def lane_pass(f, carry):
            block = pl.ds((f * ZD + base) * ROWS, size)
            val = xs[block].reshape(size * NSUB, Y)
            high = val.astype(jnp.bfloat16)
            rest = val - high.astype(jnp.float32)
            mid = rest.astype(jnp.bfloat16)
            low = (rest - mid.astype(jnp.float32)).astype(jnp.bfloat16)
            total = jnp.dot(jnp.concatenate([high, mid], axis=1), ones2, preferred_element_type=jnp.float32)
            total = total + jnp.dot(low, ones, preferred_element_type=jnp.float32)
            bx[block] = (total * (1.0 / WIN**3)).reshape(size, NSUB, Y)
            return carry

        lax.fori_loop(0, NF, lane_pass, 0)

    def combined(base, n):
        def stats(r, carry):
            for k in range(n):
                q = (base + k) * ROWS + r
                mean = bx[q]
                inv[q] = 1.0 / (bx[CELLS + q] - mean * mean + 1e-5)
                dev[q] = ext[r, RAD + base + k] - mean
            return carry

        lax.fori_loop(0, ROWS, stats, 0)
        w_flat = w_buf.reshape(NSUB * 8, 128)
        weights = [w_flat[pl.ds(r, NSUB, stride=8), :] for r in range(NREF)]

        def combine(row, carry):
            for k in range(n):
                q = (base + k) * ROWS + row
                mean_i, inv_i, dev_i = bx[q], inv[q], dev[q]
                total = None
                for r in range(NREF):
                    one = pl.ds(refs[r], 1)
                    gain = (bx[(2 + r) * CELLS + q] - mean_i * bx[q, one, :]) * inv_i
                    term = (2.0 * gain * inv[q, one, :]) * (dev[q, one, :] - gain * dev_i) * weights[r]
                    total = term if total is None else total + term
                c_buf[pl.ds((k * ROWS + row) * NSUB, NSUB), :] = total
            return carry

        lax.fori_loop(0, ROWS, combine, 0)
        for sub in range(NSUB):
            for k in range(n):
                cs[sub, base + k] = c_buf[pl.ds(k * ROWS * NSUB + sub, ROWS, stride=NSUB), :]

    def weights_end():
        for k in range(1, NSUB):
            weight_in(k).wait_recv()


    y_at, x_at = s // 4, s % 4
    pairs = [(j, i) for j in range(4) for i in range(4) if (j, i) != (0, 0)]

    def back_out(j, i, part):
        to = 4 * ((y_at + j) % 4) + (x_at + i) % 4
        base, n = parts[part]
        sem = part * NSUB + 4 * j + i
        return remote(
            cs.at[to, pl.ds(base, n)], cf.at[pl.ds(RG + base, n), c], sr.at[sem], rr.at[part * NSUB + c], (to, d)
        )

    def back_in(j, i, part):
        frm = 4 * ((y_at + 4 - j) % 4) + (x_at + 4 - i) % 4
        chunk = chunk_of(frm, hi)
        base, n = parts[part]
        sem = part * NSUB + 4 * j + i
        return remote(
            cs.at[frm, pl.ds(base, n)], cf.at[pl.ds(RG + base, n), chunk], sr.at[sem], rr.at[part * NSUB + chunk], (frm, d)
        )

    def over_up(k):
        to = peer_to(k)
        return remote(cs.at[to, pl.ds(2, RG)], cf.at[pl.ds(0, RG), c], sc.at[k], rc.at[c], (to, d + 1))

    def over_dn(k):
        to = peer_to(k)
        return remote(cs.at[to, pl.ds(0, RG)], cf.at[pl.ds(RG + ZD, RG), c], sc.at[k], rc.at[c], (to, d - 1))

    def over_in(k, first, side):
        return remote(cs.at[k, pl.ds(0, RG)], cf.at[pl.ds(first, RG), k], sc.at[k], rc.at[k], (s, side))

    def four(j):
        return pl.ds(chunk_of(4 * ((y_at + 4 - j) % 4), hi) // 4 * 4, 4)

    def f_dn(j):
        return remote(
            cf.at[pl.ds(RG, RG), four(j)], cf.at[pl.ds(RG + ZD, RG), four(j)], sh.at[FA + j], rh.at[FA + j], (s, d - 1)
        )

    def f_up(j):
        return remote(cf.at[pl.ds(ZD, RG), four(j)], cf.at[pl.ds(0, RG), four(j)], sh.at[FB + j], rh.at[FB + j], (s, d + 1))

    def home_start(part):
        if part == 0:
            @pl.when(cross_up)
            def _():
                for k in range(NSUB):
                    over_up(k).start()

        for j, i in pairs:
            back_out(j, i, part).start()

        if part == 1:
            @pl.when(cross_lo)
            def _():
                for k in range(NSUB):
                    over_dn(k).start()

        base, n = parts[part]
        cf[pl.ds(RG + base, n), c] = cs[s, pl.ds(base, n)]

    def home_end(part):
        for j in range(4):
            for i in range(4):
                if (j, i) != (0, 0):
                    back_in(j, i, part).wait_recv()

            @pl.when(near_lo & (odd == part))
            def _():
                f_dn(j).start()

            @pl.when(near_up & (odd == 1 - part))
            def _():
                f_up(j).start()

    taps = gauss_taps()
    lane = lax.broadcasted_iota(jnp.int32, (X, Y), 1)
    line = lax.broadcasted_iota(jnp.int32, (X, Y), 0)

    def plane(i):
        if i < 4:
            return ih[i].reshape(X, Y)
        if i < 4 + ZD:
            return img[i - 4].reshape(X, Y)
        return ih[i - ZD].reshape(X, Y)

    def gradients():
        @pl.when(near_lo)
        def _():
            i_up().wait_recv()

        @pl.when(near_up)
        def _():
            i_dn().wait_recv()

        @pl.when(cross_lo)
        def _():
            for k in range(1, NSUB):
                slab_in(k, 0).wait_recv()

        @pl.when(cross_up)
        def _():
            for k in range(1, NSUB):
                slab_in(k, 4).wait_recv()

        for p in range(FP):
            here = plane(p + 1)
            grad[0, p] = (plane(p + 2) - plane(p)) * 0.5
            below = jnp.where(line == X - 1, 0.0, pltpu.roll(here, X - 1, 0))
            above = jnp.where(line == 0, 0.0, pltpu.roll(here, 1, 0))
            grad[1, p] = (below - above) * 0.5
            after = jnp.where(lane == Y - 1, 0.0, pltpu.roll(here, Y - 1, 1))
            before = jnp.where(lane == 0, 0.0, pltpu.roll(here, 1, 1))
            grad[2, p] = (after - before) * 0.5

    def depth_sum(comp, p, inner):
        total = None
        for k in range(2 * RG + 1):
            q = p + k
            if (RG <= q < RG + ZD) == inner:
                term = (taps[k] * cf[q].reshape(X, Y)) * grad[comp, q]
                total = term if total is None else total + term
        return total

    def inner_part():
        def body(comp, carry):
            for p in range(ZD):
                part[comp, p] = depth_sum(comp, p, True)
            return carry

        lax.fori_loop(0, 3, body, 0)

    def outer_part():
        matrix = band(taps, jnp.float32)
        t_high = matrix.astype(jnp.bfloat16)
        t_low = (matrix - t_high.astype(jnp.float32)).astype(jnp.bfloat16)
        none = jnp.zeros((128, 128), jnp.bfloat16)
        right = jnp.concatenate(
            [jnp.concatenate([t_high, t_low], axis=1), jnp.concatenate([t_high, none], axis=1)], axis=0
        )
        left = jnp.concatenate(
            [jnp.concatenate([t_high, t_high], axis=1), jnp.concatenate([t_low, none], axis=1)], axis=0
        )

        def split(val):
            high = val.astype(jnp.bfloat16)
            return high, (val - high.astype(jnp.float32)).astype(jnp.bfloat16)

        def body(first, last, comp, carry):
            for p in range(first, last):
                total = part[comp, p] + depth_sum(comp, p, False)
                both = jnp.dot(jnp.concatenate(split(total), axis=1), right, preferred_element_type=jnp.float32)
                across = both[:, :Y] + both[:, Y:]
                both = jnp.dot(left, jnp.concatenate(split(across), axis=0), preferred_element_type=jnp.float32)
                out[comp, p] = 40.0 * (both[:X] + both[X:])
            return carry

        @pl.when(near_up)
        def _():
            for j in range(4):
                f_dn(j).wait_recv()

        @pl.when(cross_up)
        def _():
            for k in range(NSUB):
                over_in(k, RG + ZD, d + 1).wait_recv()

        lax.fori_loop(0, 3, functools.partial(body, RG, ZD), 0)

        @pl.when(near_lo)
        def _():
            for j in range(4):
                f_up(j).wait_recv()

        @pl.when(cross_lo)
        def _():
            for k in range(NSUB):
                over_in(k, 0, d - 1).wait_recv()

        lax.fori_loop(0, 3, functools.partial(body, 0, RG), 0)

    def halo_drain():
        @pl.when(has_prev)
        def _():
            x_dn(core_p, XA, XA).wait_send()

        @pl.when(has_next)
        def _():
            x_up(core_p, XB, XB).wait_send()

        across_dn_x(lambda copy: copy.wait_send())
        across_up_x(lambda copy: copy.wait_send())

        @pl.when(near_lo)
        def _():
            i_dn().wait_send()
            z_dn(ext, ZA).wait_send()

            @pl.when(has_prev)
            def _():
                z_dn(ext_top, CA0).wait_send()

            @pl.when(has_next)
            def _():
                z_dn(ext_bot, CA1).wait_send()

        @pl.when(near_up)
        def _():
            i_up().wait_send()
            z_up(ext, ZB).wait_send()

            @pl.when(has_prev)
            def _():
                z_up(ext_top, CB0).wait_send()

            @pl.when(has_next)
            def _():
                z_up(ext_bot, CB1).wait_send()

    def slab_drain():
        def both(first):
            for k in range(1, NSUB):
                slab_out(k, first).wait_send()

        @pl.when(cross_lo)
        def _():
            both(0)

        @pl.when(cross_up)
        def _():
            both(4)

    def spread_drain():
        for k in range(1, NSUB):
            chunk_out(k).wait_send()
            weight_out(k).wait_send()

        @pl.when(cross_up)
        def _():
            for k in range(NSUB):
                far_out(k, 1, d + 1).wait_send()

        @pl.when(cross_lo)
        def _():
            for k in range(NSUB):
                far_out(k, 0, d - 1).wait_send()

    def home_drain():
        for j, i in pairs:
            back_out(j, i, 0).wait_send()
            back_out(j, i, 1).wait_send()

        @pl.when(cross_up)
        def _():
            for k in range(NSUB):
                over_up(k).wait_send()

        @pl.when(cross_lo)
        def _():
            for k in range(NSUB):
                over_dn(k).wait_send()

        @pl.when(near_lo)
        def _():
            for j in range(4):
                f_dn(j).wait_send()

        @pl.when(near_up)
        def _():
            for j in range(4):
                f_up(j).wait_send()

    spread()
    halo_start()
    slabs()
    core_rows()
    corners_end()
    other_rows()
    weights_end()
    for turn in range(2):
        boxes(*parts[turn])
        combined(*parts[turn])
        home_start(turn)
    gradients()
    spread_drain()
    halo_drain()
    slab_drain()
    home_end(0)
    home_end(1)
    inner_part()
    outer_part()
    home_drain()


def on_device(images, velocity, ref_index, ref_weights):
    vmem = pl.BlockSpec(memory_space=pltpu.VMEM)
    smem = pl.BlockSpec(memory_space=pltpu.SMEM)
    f32 = jnp.float32
    dma = pltpu.SemaphoreType.DMA
    smooth = pl.pallas_call(
        coeff_kernel,
        out_shape=jax.ShapeDtypeStruct((3, ZD, X, Y), f32),
        in_specs=[smem, smem, pl.BlockSpec(memory_space=pltpu.HBM)],
        out_specs=vmem,
        scratch_shapes=[
            pltpu.VMEM((ZD, NSUB, ROWS, Y), f32),
            pltpu.VMEM((NSUB, ZD, ROWS, Y), f32),
            pltpu.VMEM((NSUB, 8, 128), f32),
            pltpu.VMEM((ROWS, EXT_P, NSUB, Y), f32),
            pltpu.VMEM((RAD, EXT_P, NSUB, Y), f32),
            pltpu.VMEM((RAD, EXT_P, NSUB, Y), f32),
            pltpu.VMEM((NF, EXT_R, ZD, NSUB, Y), f32),
            pltpu.VMEM((NF * CELLS, NSUB, Y), f32),
            pltpu.VMEM((NF * CELLS, NSUB, Y), f32),
            pltpu.VMEM((CELLS, NSUB, Y), f32),
            pltpu.VMEM((CELLS, NSUB, Y), f32),
            pltpu.VMEM((CELLS * NSUB, Y), f32),
            pltpu.VMEM((NSUB, ZD, ROWS, Y), f32),
            pltpu.VMEM((NSUB, 4, ROWS, Y), f32),
            pltpu.VMEM((FP, NSUB, ROWS, Y), f32),
            pltpu.VMEM((8, NSUB, ROWS, Y), f32),
            pltpu.VMEM((3, FP, X, Y), f32),
            pltpu.VMEM((3, ZD, X, Y), f32),
            dma((NSUB,)), dma((NSUB,)), dma((NSUB,)), dma((NSUB,)), dma((2 * NSUB,)), dma((2 * NSUB,)),
            dma((NSUB,)), dma((NSUB,)), dma((NSUB,)), dma((NSUB,)), dma((NSUB,)), dma((NSUB,)),
            dma((20,)), dma((20,)), dma,
        ],
        compiler_params=pltpu.CompilerParams(
            collective_id=0, has_side_effects=True, vmem_limit_bytes=VLIM * 1024 * 1024
        ),
    )(pltpu.with_memory_space_constraint(ref_index, pltpu.HBM), pltpu.with_memory_space_constraint(ref_weights, pltpu.HBM), pltpu.with_memory_space_constraint(images.reshape(ZD, NSUB, ROWS, Y), pltpu.HBM))
    return velocity + smooth.reshape(3, 1, ZD, X, Y)


def solution(mesh):
    placed = (
        P("subj", "depth", None, None),
        P(None, "subj", "depth", None, None),
        P(),
        P("subj", None),
    )
    return jax.shard_map(
        on_device,
        mesh=mesh,
        in_specs=placed,
        out_specs=P(None, "subj", "depth", None, None),
        check_vma=False,
    )
```

```python
import functools
import math

import jax
import jax.numpy as jnp
from jax import lax
from jax.experimental import pallas as pl
from jax.experimental.pallas import tpu as pltpu
from jax.sharding import PartitionSpec as P

X = 128
Y = 128
ZD = 5
NSUB = 16
NREF = 4
WIN = 9
RG = 3
WDEN = 16
RAD = WIN // 2
ROWS = X // NSUB
EXT_R = ROWS + 2 * RAD
EXT_P = ZD + 2 * RAD
CELLS = ROWS * ZD
NF = 2 + NREF
FP = ZD + 2 * RG
VLIM = 32
ORDER = (4, 12, 8, 5, 13, 9, 6, 14, 10, 7, 15, 11, 1, 3, 2)
MESH = pl.DeviceIdType.MESH

XA, XB, ZA, ZB, CA0, CA1, CB0, CB1, IA, IB, YA, YB, FA, FB = list(range(13)) + [16]


def gauss_taps():
    raw = [math.exp(-0.5 * offset * offset) for offset in range(-RG, RG + 1)]
    total = sum(raw)
    return [value / total for value in raw]


def chunk_of(s, hi):
    y, x = s // 4, s % 4
    ys = y + hi * (3 - 2 * y)
    return 4 * ys + x + (ys % 2) * (3 - 2 * x)


def subject_of(c, hi):
    ys, xs = c // 4, c % 4
    x = xs + (ys % 2) * (3 - 2 * xs)
    return 4 * (ys + hi * (3 - 2 * ys)) + x


def window_depth(v):
    core = ((v[4] + v[5]) + (v[6] + v[7])) + v[8]
    suf2 = v[2] + v[3]
    suf1 = v[1] + suf2
    suf0 = v[0] + suf1
    pre2 = v[9] + v[10]
    pre3 = pre2 + v[11]
    pre4 = pre3 + v[12]
    return [core + suf0, (core + suf1) + v[9], (core + suf2) + pre2, (core + v[3]) + pre3, core + pre4]


def window_rows(v):
    suf = [None] * 8
    pre = [None] * 8
    suf[7] = v[7]
    pre[0] = v[8]
    for i in range(6, -1, -1):
        suf[i] = v[i] + suf[i + 1]
    for i in range(1, 8):
        pre[i] = pre[i - 1] + v[8 + i]
    return [suf[i] + pre[i] for i in range(8)]


def band(taps, dtype):
    radius = len(taps) // 2
    diff = lax.broadcasted_iota(jnp.int32, (128, 128), 0) - lax.broadcasted_iota(jnp.int32, (128, 128), 1)
    matrix = jnp.zeros((128, 128), jnp.float32)
    for offset in range(len(taps)):
        matrix = jnp.where(diff == offset - radius, taps[offset], matrix)
    return matrix.astype(dtype)


def coeff_kernel(
    idx_ref, w_ref, img_hbm, out,
    img, a_buf, w_buf, ext, ext_top, ext_bot, zs, xs, bx, inv, dev, c_buf, cs, b_buf, cf, ih, grad, part,
    sa, ra, sw, rw, sr, rr, sb, rb, sg, rg, sc, rc, sh, rh, load_sem,
):
    s = lax.axis_index("subj")
    d = lax.axis_index("depth")
    nd = lax.axis_size("depth")
    half = nd // 2
    hi = d // half
    c = chunk_of(s, hi)
    has_lo, has_up = d > 0, d < nd - 1
    cross_lo, cross_up = d == half, d == half - 1
    near_lo, near_up = has_lo & (d != half), has_up & (d != half - 1)
    has_prev, has_next = c > 0, c < NSUB - 1
    load = pltpu.make_async_copy(img_hbm, img, load_sem)
    load.start()

    barrier = pltpu.get_barrier_semaphore()
    for k in range(1, NSUB):
        pl.semaphore_signal(barrier, inc=1, device_id=((s + k) % NSUB, d), device_id_type=MESH)

    @pl.when(near_lo)
    def _():
        pl.semaphore_signal(barrier, inc=1, device_id=(s, d - 1), device_id_type=MESH)

    @pl.when(near_up)
    def _():
        pl.semaphore_signal(barrier, inc=1, device_id=(s, d + 1), device_id_type=MESH)

    @pl.when(cross_lo)
    def _():
        for k in range(NSUB):
            pl.semaphore_signal(barrier, inc=1, device_id=((s + k) % NSUB, d - 1), device_id_type=MESH)

    @pl.when(cross_up)
    def _():
        for k in range(NSUB):
            pl.semaphore_signal(barrier, inc=1, device_id=((s + k) % NSUB, d + 1), device_id_type=MESH)

    rows = lax.broadcasted_iota(jnp.int32, (8, 128), 0)
    wt = jnp.zeros((8, 128), jnp.float32)
    for r in range(NREF):
        wt = jnp.where(rows == r, w_ref[0, r].astype(jnp.float32) * (1.0 / WDEN), wt)
    w_buf[s] = wt

    @pl.when(c == 0)
    def _():
        ext_top[...] = jnp.zeros((RAD, EXT_P, NSUB, Y), jnp.float32)

    @pl.when(c == NSUB - 1)
    def _():
        ext_bot[...] = jnp.zeros((RAD, EXT_P, NSUB, Y), jnp.float32)

    @pl.when(jnp.logical_not(has_lo))
    def _():
        ext[:, 0:RAD] = jnp.zeros((ROWS, RAD, NSUB, Y), jnp.float32)
        ext_top[:, 0:RAD] = jnp.zeros((RAD, RAD, NSUB, Y), jnp.float32)
        ext_bot[:, 0:RAD] = jnp.zeros((RAD, RAD, NSUB, Y), jnp.float32)
        ih[0:4] = jnp.zeros((4, NSUB, ROWS, Y), jnp.float32)
        cf[0:RG] = jnp.zeros((RG, NSUB, ROWS, Y), jnp.float32)

    @pl.when(jnp.logical_not(has_up))
    def _():
        ext[:, RAD + ZD:] = jnp.zeros((ROWS, RAD, NSUB, Y), jnp.float32)
        ext_top[:, RAD + ZD:] = jnp.zeros((RAD, RAD, NSUB, Y), jnp.float32)
        ext_bot[:, RAD + ZD:] = jnp.zeros((RAD, RAD, NSUB, Y), jnp.float32)
        ih[4:8] = jnp.zeros((4, NSUB, ROWS, Y), jnp.float32)
        cf[RG + ZD:] = jnp.zeros((RG, NSUB, ROWS, Y), jnp.float32)

    load.wait()
    one_if = lambda cond: cond.astype(jnp.int32)
    extra = one_if(near_lo) + one_if(near_up) + NSUB * (one_if(cross_lo) + one_if(cross_up))
    pl.semaphore_wait(barrier, NSUB - 1 + extra)

    def remote(src, dst, send, recv, device):
        return pltpu.make_async_remote_copy(
            src_ref=src, dst_ref=dst, send_sem=send, recv_sem=recv, device_id=device, device_id_type=MESH
        )

    def peer_to(k):
        return (s + k) % NSUB

    def peer_from(k):
        return (s + NSUB - k) % NSUB

    def chunk_out(k):
        to = peer_to(k)
        return remote(img.at[:, chunk_of(to, hi)], a_buf.at[s], sa.at[k], ra.at[s], (to, d))

    def chunk_in(k):
        frm = peer_from(k)
        return remote(img.at[:, 0], a_buf.at[frm], sa.at[k], ra.at[frm], (frm, d))

    def weight_out(k):
        return remote(w_buf.at[s], w_buf.at[s], sw.at[k], rw.at[s], (peer_to(k), d))

    def weight_in(k):
        frm = peer_from(k)
        return remote(w_buf.at[frm], w_buf.at[frm], sw.at[k], rw.at[frm], (frm, d))

    def far_out(k, first, side):
        to = peer_to(k)
        return remote(img.at[pl.ds(first, 4), chunk_of(to, 1 - hi)], b_buf.at[s], sb.at[k], rb.at[s], (to, side))

    def far_in(k, side):
        return remote(b_buf.at[k], b_buf.at[k], sb.at[k], rb.at[k], (s, side))

    def spread():
        for k in ORDER:
            chunk_out(k).start()

        @pl.when(cross_up)
        def _():
            for k in range(NSUB):
                far_out(k, 1, d + 1).start()

        @pl.when(cross_lo)
        def _():
            for k in range(NSUB):
                far_out(k, 0, d - 1).start()

        a_buf[s] = img[:, c]
        for k in range(1, NSUB):
            chunk_in(k).wait_recv()
        a_flat = a_buf.reshape(NSUB * ZD * ROWS, Y)
        for p in range(ZD):
            for r in range(ROWS):
                ext[r, RAD + p] = a_flat[pl.ds(p * ROWS + r, NSUB, stride=ZD * ROWS), :]

    prev, nxt = subject_of(jnp.maximum(c - 1, 0), hi), subject_of(jnp.minimum(c + 1, NSUB - 1), hi)
    core_p = pl.ds(RAD, ZD)
    low_p, high_p = pl.ds(0, RAD), pl.ds(RAD + ZD, RAD)

    def x_dn(planes, send, recv):
        return remote(ext.at[pl.ds(0, RAD), planes], ext_bot.at[:, planes], sh.at[send], rh.at[recv], (prev, d))

    def x_up(planes, send, recv):
        return remote(ext.at[pl.ds(RAD, RAD), planes], ext_top.at[:, planes], sh.at[send], rh.at[recv], (nxt, d))

    def z_dn(block, sem):
        return remote(block.at[:, pl.ds(RAD, RAD)], block.at[:, high_p], sh.at[sem], rh.at[sem], (s, d - 1))

    def z_up(block, sem):
        return remote(block.at[:, pl.ds(ZD, RAD)], block.at[:, low_p], sh.at[sem], rh.at[sem], (s, d + 1))

    def i_dn():
        return remote(img.at[pl.ds(0, 4)], ih.at[pl.ds(4, 4)], sh.at[IA], rh.at[IA], (s, d - 1))

    def i_up():
        return remote(img.at[pl.ds(1, 4)], ih.at[pl.ds(0, 4)], sh.at[IB], rh.at[IB], (s, d + 1))

    def across_dn_x(go):
        @pl.when(has_prev)
        def _():
            @pl.when(cross_up)
            def _():
                go(x_dn(high_p, YA, CA1))

            @pl.when(cross_lo)
            def _():
                go(x_dn(low_p, YA, CB1))

    def across_up_x(go):
        @pl.when(has_next)
        def _():
            @pl.when(cross_up)
            def _():
                go(x_up(high_p, YB, CA0))

            @pl.when(cross_lo)
            def _():
                go(x_up(low_p, YB, CB0))

    def halo_start():
        @pl.when(near_lo)
        def _():
            z_dn(ext, ZA).start()

        @pl.when(near_up)
        def _():
            z_up(ext, ZB).start()

        @pl.when(has_prev)
        def _():
            x_dn(core_p, XA, XA).start()

        @pl.when(has_next)
        def _():
            x_up(core_p, XB, XB).start()

        for k in range(1, NSUB):
            weight_out(k).start()

        @pl.when(has_next)
        def _():
            x_dn(core_p, XA, XA).wait_recv()

            @pl.when(near_lo)
            def _():
                z_dn(ext_bot, CA1).start()

            @pl.when(near_up)
            def _():
                z_up(ext_bot, CB1).start()

        @pl.when(has_prev)
        def _():
            x_up(core_p, XB, XB).wait_recv()

            @pl.when(near_lo)
            def _():
                z_dn(ext_top, CA0).start()

            @pl.when(near_up)
            def _():
                z_up(ext_top, CB0).start()

        b_flat = b_buf.reshape(NSUB * 4 * ROWS, Y)

        def far_end(side, base):
            for k in range(NSUB):
                far_in(k, side).wait_recv()
            for p in range(4):
                for r in range(ROWS):
                    ext[r, base + p] = b_flat[pl.ds(p * ROWS + r, NSUB, stride=4 * ROWS), :]

        @pl.when(cross_lo)
        def _():
            far_end(d - 1, 0)

        @pl.when(cross_up)
        def _():
            far_end(d + 1, RAD + ZD)

        across_dn_x(lambda copy: copy.start())
        across_up_x(lambda copy: copy.start())

        @pl.when(near_up)
        def _():
            z_dn(ext, ZA).wait_recv()

        @pl.when(near_lo)
        def _():
            z_up(ext, ZB).wait_recv()

        @pl.when(near_lo)
        def _():
            i_dn().start()

        @pl.when(near_up)
        def _():
            i_up().start()

    def slab_out(k, first):
        to = peer_to(k)
        return remote(b_buf.at[to], ih.at[pl.ds(first, 4), c], sg.at[k], rg.at[c], (to, d))

    def slab_in(k, first):
        frm = peer_from(k)
        chunk = chunk_of(frm, hi)
        return remote(b_buf.at[frm], ih.at[pl.ds(first, 4), chunk], sg.at[k], rg.at[chunk], (frm, d))

    def slab_start(first):
        for k in range(1, NSUB):
            slab_out(k, first).start()
        ih[pl.ds(first, 4), c] = b_buf[s]

    def slabs():
        @pl.when(cross_lo)
        def _():
            slab_start(0)

        @pl.when(cross_up)
        def _():
            slab_start(4)

    def corners_end():
        @pl.when(has_up)
        def _():
            @pl.when(has_prev)
            def _():
                z_dn(ext_top, CA0).wait_recv()

            @pl.when(has_next)
            def _():
                z_dn(ext_bot, CA1).wait_recv()

        @pl.when(has_lo)
        def _():
            @pl.when(has_prev)
            def _():
                z_up(ext_top, CB0).wait_recv()

            @pl.when(has_next)
            def _():
                z_up(ext_bot, CB1).wait_recv()

    refs = [idx_ref[r] for r in range(NREF)]

    def depth_pass(block, first, row, carry):
        at = row + first
        vals = [block[row, p] for p in range(EXT_P)]
        for k, total in enumerate(window_depth(vals)):
            zs[0, at, k] = total
        for k, total in enumerate(window_depth([v * v for v in vals])):
            zs[1, at, k] = total
        for r in range(NREF):
            prods = [vals[p] * block[row, p, pl.ds(refs[r], 1), :] for p in range(EXT_P)]
            for k, total in enumerate(window_depth(prods)):
                zs[2 + r, at, k] = total
        return carry

    odd = d % 2
    parts = ((2 * odd, 3), (3 - 3 * odd, 2))

    def row_pass(base, n, f, carry):
        for k in range(n):
            at = base + k
            for r, total in enumerate(window_rows([zs[f, row, at] for row in range(EXT_R)])):
                xs[(f * ZD + at) * ROWS + r] = total
        return carry

    def core_rows():
        lax.fori_loop(0, ROWS, functools.partial(depth_pass, ext, RAD), 0)

    def other_rows():
        lax.fori_loop(0, RAD, functools.partial(depth_pass, ext_top, 0), 0)
        lax.fori_loop(0, RAD, functools.partial(depth_pass, ext_bot, RAD + ROWS), 0)

    def boxes(base, n):
        lax.fori_loop(0, NF, functools.partial(row_pass, base, n), 0)
        ones = band([1.0] * WIN, jnp.bfloat16)
        ones2 = jnp.concatenate([ones, ones], axis=0)
        size = n * ROWS

        def lane_pass(f, carry):
            block = pl.ds((f * ZD + base) * ROWS, size)
            val = xs[block].reshape(size * NSUB, Y)
            high = val.astype(jnp.bfloat16)
            rest = val - high.astype(jnp.float32)
            mid = rest.astype(jnp.bfloat16)
            low = (rest - mid.astype(jnp.float32)).astype(jnp.bfloat16)
            total = jnp.dot(jnp.concatenate([high, mid], axis=1), ones2, preferred_element_type=jnp.float32)
            total = total + jnp.dot(low, ones, preferred_element_type=jnp.float32)
            bx[block] = (total * (1.0 / WIN**3)).reshape(size, NSUB, Y)
            return carry

        lax.fori_loop(0, NF, lane_pass, 0)

    def combined(base, n):
        def stats(r, carry):
            for k in range(n):
                q = (base + k) * ROWS + r
                mean = bx[q]
                inv[q] = 1.0 / (bx[CELLS + q] - mean * mean + 1e-5)
                dev[q] = ext[r, RAD + base + k] - mean
            return carry

        lax.fori_loop(0, ROWS, stats, 0)
        w_flat = w_buf.reshape(NSUB * 8, 128)
        weights = [w_flat[pl.ds(r, NSUB, stride=8), :] for r in range(NREF)]

        def combine(row, carry):
            for k in range(n):
                q = (base + k) * ROWS + row
                mean_i, inv_i, dev_i = bx[q], inv[q], dev[q]
                total = None
                for r in range(NREF):
                    one = pl.ds(refs[r], 1)
                    gain = (bx[(2 + r) * CELLS + q] - mean_i * bx[q, one, :]) * inv_i
                    term = (2.0 * gain * inv[q, one, :]) * (dev[q, one, :] - gain * dev_i) * weights[r]
                    total = term if total is None else total + term
                c_buf[pl.ds((k * ROWS + row) * NSUB, NSUB), :] = total
            return carry

        lax.fori_loop(0, ROWS, combine, 0)
        for sub in range(NSUB):
            for k in range(n):
                cs[sub, base + k] = c_buf[pl.ds(k * ROWS * NSUB + sub, ROWS, stride=NSUB), :]

    def weights_end():
        for k in range(1, NSUB):
            weight_in(k).wait_recv()


    y_at, x_at = s // 4, s % 4
    pairs = [(j, i) for j in range(4) for i in range(4) if (j, i) != (0, 0)]

    def back_out(j, i, part):
        to = 4 * ((y_at + j) % 4) + (x_at + i) % 4
        base, n = parts[part]
        sem = part * NSUB + 4 * j + i
        return remote(
            cs.at[to, pl.ds(base, n)], cf.at[pl.ds(RG + base, n), c], sr.at[sem], rr.at[part * NSUB + c], (to, d)
        )

    def back_in(j, i, part):
        frm = 4 * ((y_at + 4 - j) % 4) + (x_at + 4 - i) % 4
        chunk = chunk_of(frm, hi)
        base, n = parts[part]
        sem = part * NSUB + 4 * j + i
        return remote(
            cs.at[frm, pl.ds(base, n)], cf.at[pl.ds(RG + base, n), chunk], sr.at[sem], rr.at[part * NSUB + chunk], (frm, d)
        )

    def over_up(k):
        to = peer_to(k)
        return remote(cs.at[to, pl.ds(2, RG)], cf.at[pl.ds(0, RG), c], sc.at[k], rc.at[c], (to, d + 1))

    def over_dn(k):
        to = peer_to(k)
        return remote(cs.at[to, pl.ds(0, RG)], cf.at[pl.ds(RG + ZD, RG), c], sc.at[k], rc.at[c], (to, d - 1))

    def over_in(k, first, side):
        return remote(cs.at[k, pl.ds(0, RG)], cf.at[pl.ds(first, RG), k], sc.at[k], rc.at[k], (s, side))

    def four(j):
        return pl.ds(chunk_of(4 * ((y_at + 4 - j) % 4), hi) // 4 * 4, 4)

    def f_dn(j):
        return remote(
            cf.at[pl.ds(RG, RG), four(j)], cf.at[pl.ds(RG + ZD, RG), four(j)], sh.at[FA + j], rh.at[FA + j], (s, d - 1)
        )

    def f_up(j):
        return remote(cf.at[pl.ds(ZD, RG), four(j)], cf.at[pl.ds(0, RG), four(j)], sh.at[FB + j], rh.at[FB + j], (s, d + 1))

    def home_start(part):
        if part == 0:
            @pl.when(cross_up)
            def _():
                for k in (8, 9, 10, 11, 7, 6, 5, 4, 12, 13, 14, 15, 0, 1, 2, 3):
                    over_up(k).start()

        for j, i in pairs:
            back_out(j, i, part).start()

        if part == 1:
            @pl.when(cross_lo)
            def _():
                for k in range(NSUB):
                    over_dn(k).start()

        base, n = parts[part]
        cf[pl.ds(RG + base, n), c] = cs[s, pl.ds(base, n)]

    def home_end(part):
        for j in range(4):
            for i in range(4):
                if (j, i) != (0, 0):
                    back_in(j, i, part).wait_recv()

            @pl.when(near_lo & (odd == part))
            def _():
                f_dn(j).start()

            @pl.when(near_up & (odd == 1 - part))
            def _():
                f_up(j).start()

    taps = gauss_taps()
    lane = lax.broadcasted_iota(jnp.int32, (X, Y), 1)
    line = lax.broadcasted_iota(jnp.int32, (X, Y), 0)

    def plane(i):
        if i < 4:
            return ih[i].reshape(X, Y)
        if i < 4 + ZD:
            return img[i - 4].reshape(X, Y)
        return ih[i - ZD].reshape(X, Y)

    def gradients():
        @pl.when(near_lo)
        def _():
            i_up().wait_recv()

        @pl.when(near_up)
        def _():
            i_dn().wait_recv()

        @pl.when(cross_lo)
        def _():
            for k in range(1, NSUB):
                slab_in(k, 0).wait_recv()

        @pl.when(cross_up)
        def _():
            for k in range(1, NSUB):
                slab_in(k, 4).wait_recv()

        for p in range(FP):
            here = plane(p + 1)
            grad[0, p] = (plane(p + 2) - plane(p)) * 0.5
            below = jnp.where(line == X - 1, 0.0, pltpu.roll(here, X - 1, 0))
            above = jnp.where(line == 0, 0.0, pltpu.roll(here, 1, 0))
            grad[1, p] = (below - above) * 0.5
            after = jnp.where(lane == Y - 1, 0.0, pltpu.roll(here, Y - 1, 1))
            before = jnp.where(lane == 0, 0.0, pltpu.roll(here, 1, 1))
            grad[2, p] = (after - before) * 0.5

    def depth_sum(comp, p, inner):
        total = None
        for k in range(2 * RG + 1):
            q = p + k
            if (RG <= q < RG + ZD) == inner:
                term = (taps[k] * cf[q].reshape(X, Y)) * grad[comp, q]
                total = term if total is None else total + term
        return total

    def inner_part():
        def body(comp, carry):
            for p in range(ZD):
                part[comp, p] = depth_sum(comp, p, True)
            return carry

        lax.fori_loop(0, 3, body, 0)

    def outer_part():
        matrix = band(taps, jnp.float32)
        t_high = matrix.astype(jnp.bfloat16)
        t_low = (matrix - t_high.astype(jnp.float32)).astype(jnp.bfloat16)
        none = jnp.zeros((128, 128), jnp.bfloat16)
        right = jnp.concatenate(
            [jnp.concatenate([t_high, t_low], axis=1), jnp.concatenate([t_high, none], axis=1)], axis=0
        )
        left = jnp.concatenate(
            [jnp.concatenate([t_high, t_high], axis=1), jnp.concatenate([t_low, none], axis=1)], axis=0
        )

        def split(val):
            high = val.astype(jnp.bfloat16)
            return high, (val - high.astype(jnp.float32)).astype(jnp.bfloat16)

        def body(first, last, comp, carry):
            for p in range(first, last):
                total = part[comp, p] + depth_sum(comp, p, False)
                both = jnp.dot(jnp.concatenate(split(total), axis=1), right, preferred_element_type=jnp.float32)
                across = both[:, :Y] + both[:, Y:]
                both = jnp.dot(left, jnp.concatenate(split(across), axis=0), preferred_element_type=jnp.float32)
                out[comp, p] = 40.0 * (both[:X] + both[X:])
            return carry

        @pl.when(near_up)
        def _():
            for j in range(4):
                f_dn(j).wait_recv()

        @pl.when(cross_up)
        def _():
            for k in range(NSUB):
                over_in(k, RG + ZD, d + 1).wait_recv()

        lax.fori_loop(0, 3, functools.partial(body, RG, ZD), 0)

        @pl.when(near_lo)
        def _():
            for j in range(4):
                f_up(j).wait_recv()

        @pl.when(cross_lo)
        def _():
            for k in range(NSUB):
                over_in(k, 0, d - 1).wait_recv()

        lax.fori_loop(0, 3, functools.partial(body, 0, RG), 0)

    def halo_drain():
        @pl.when(has_prev)
        def _():
            x_dn(core_p, XA, XA).wait_send()

        @pl.when(has_next)
        def _():
            x_up(core_p, XB, XB).wait_send()

        across_dn_x(lambda copy: copy.wait_send())
        across_up_x(lambda copy: copy.wait_send())

        @pl.when(near_lo)
        def _():
            i_dn().wait_send()
            z_dn(ext, ZA).wait_send()

            @pl.when(has_prev)
            def _():
                z_dn(ext_top, CA0).wait_send()

            @pl.when(has_next)
            def _():
                z_dn(ext_bot, CA1).wait_send()

        @pl.when(near_up)
        def _():
            i_up().wait_send()
            z_up(ext, ZB).wait_send()

            @pl.when(has_prev)
            def _():
                z_up(ext_top, CB0).wait_send()

            @pl.when(has_next)
            def _():
                z_up(ext_bot, CB1).wait_send()

    def slab_drain():
        def both(first):
            for k in range(1, NSUB):
                slab_out(k, first).wait_send()

        @pl.when(cross_lo)
        def _():
            both(0)

        @pl.when(cross_up)
        def _():
            both(4)

    def spread_drain():
        for k in range(1, NSUB):
            chunk_out(k).wait_send()
            weight_out(k).wait_send()

        @pl.when(cross_up)
        def _():
            for k in range(NSUB):
                far_out(k, 1, d + 1).wait_send()

        @pl.when(cross_lo)
        def _():
            for k in range(NSUB):
                far_out(k, 0, d - 1).wait_send()

    def home_drain():
        for j, i in pairs:
            back_out(j, i, 0).wait_send()
            back_out(j, i, 1).wait_send()

        @pl.when(cross_up)
        def _():
            for k in range(NSUB):
                over_up(k).wait_send()

        @pl.when(cross_lo)
        def _():
            for k in range(NSUB):
                over_dn(k).wait_send()

        @pl.when(near_lo)
        def _():
            for j in range(4):
                f_dn(j).wait_send()

        @pl.when(near_up)
        def _():
            for j in range(4):
                f_up(j).wait_send()

    spread()
    halo_start()
    slabs()
    core_rows()
    corners_end()
    other_rows()
    weights_end()
    for turn in range(2):
        boxes(*parts[turn])
        combined(*parts[turn])
        home_start(turn)
    gradients()
    spread_drain()
    halo_drain()
    slab_drain()
    home_end(0)
    home_end(1)
    inner_part()
    outer_part()
    home_drain()


def on_device(images, velocity, ref_index, ref_weights):
    vmem = pl.BlockSpec(memory_space=pltpu.VMEM)
    smem = pl.BlockSpec(memory_space=pltpu.SMEM)
    f32 = jnp.float32
    dma = pltpu.SemaphoreType.DMA
    smooth = pl.pallas_call(
        coeff_kernel,
        out_shape=jax.ShapeDtypeStruct((3, ZD, X, Y), f32),
        in_specs=[smem, smem, pl.BlockSpec(memory_space=pltpu.HBM)],
        out_specs=vmem,
        scratch_shapes=[
            pltpu.VMEM((ZD, NSUB, ROWS, Y), f32),
            pltpu.VMEM((NSUB, ZD, ROWS, Y), f32),
            pltpu.VMEM((NSUB, 8, 128), f32),
            pltpu.VMEM((ROWS, EXT_P, NSUB, Y), f32),
            pltpu.VMEM((RAD, EXT_P, NSUB, Y), f32),
            pltpu.VMEM((RAD, EXT_P, NSUB, Y), f32),
            pltpu.VMEM((NF, EXT_R, ZD, NSUB, Y), f32),
            pltpu.VMEM((NF * CELLS, NSUB, Y), f32),
            pltpu.VMEM((NF * CELLS, NSUB, Y), f32),
            pltpu.VMEM((CELLS, NSUB, Y), f32),
            pltpu.VMEM((CELLS, NSUB, Y), f32),
            pltpu.VMEM((CELLS * NSUB, Y), f32),
            pltpu.VMEM((NSUB, ZD, ROWS, Y), f32),
            pltpu.VMEM((NSUB, 4, ROWS, Y), f32),
            pltpu.VMEM((FP, NSUB, ROWS, Y), f32),
            pltpu.VMEM((8, NSUB, ROWS, Y), f32),
            pltpu.VMEM((3, FP, X, Y), f32),
            pltpu.VMEM((3, ZD, X, Y), f32),
            dma((NSUB,)), dma((NSUB,)), dma((NSUB,)), dma((NSUB,)), dma((2 * NSUB,)), dma((2 * NSUB,)),
            dma((NSUB,)), dma((NSUB,)), dma((NSUB,)), dma((NSUB,)), dma((NSUB,)), dma((NSUB,)),
            dma((20,)), dma((20,)), dma,
        ],
        compiler_params=pltpu.CompilerParams(
            collective_id=0, has_side_effects=True, vmem_limit_bytes=VLIM * 1024 * 1024
        ),
    )(pltpu.with_memory_space_constraint(ref_index, pltpu.HBM), pltpu.with_memory_space_constraint(ref_weights, pltpu.HBM), pltpu.with_memory_space_constraint(images.reshape(ZD, NSUB, ROWS, Y), pltpu.HBM))
    return velocity + smooth.reshape(3, 1, ZD, X, Y)


def solution(mesh):
    placed = (
        P("subj", "depth", None, None),
        P(None, "subj", "depth", None, None),
        P(),
        P("subj", None),
    )
    return jax.shard_map(
        on_device,
        mesh=mesh,
        in_specs=placed,
        out_specs=P(None, "subj", "depth", None, None),
        check_vma=False,
    )
```
